32 devices in a mesh: fsdp: 8 (over z, x), rep: 4 (over y, core).
Axes of the slice: x: 2, y: 2, z: 4, core: 2. Of those that a mesh axis runs over, the one named last changes fastest.
Arguments:
- inputs: bfloat16 [256, 14, 14, 512], P(('fsdp', 'rep')), may hold values from -6 to 6
- cotangent: bfloat16 [256, 14, 14, 512], P(('fsdp', 'rep')), may hold values from -6 to 6
- image_counts: int32 [8, 4], P('fsdp', 'rep'), may hold values from 1 to 8, as said below
- region_labels: int32 [4, 49], replicated, may hold values from 0 to 3
- position_index: int32 [49, 49], replicated, may hold values from 0 to 168
- first_gain: bfloat16 [512], P('fsdp'), may hold values from 0.25 to 1.75
- first_shift: bfloat16 [512], P('fsdp'), may hold values from -3 to 3
- attend_weight: bfloat16 [512, 1536], P('fsdp'), may hold values from -0.25 to 0.25
- attend_bias: bfloat16 [1024], P('fsdp'), may hold values from -3 to 3
- bias_table: bfloat16 [169, 16], replicated, may hold values from -4 to 4
- output_weight: bfloat16 [512, 512], P('fsdp'), may hold values from -1 to 1
- output_bias: bfloat16 [512], P('fsdp'), may hold values from -3 to 3
- second_gain: bfloat16 [512], P('fsdp'), may hold values from 0.25 to 1.75
- second_shift: bfloat16 [512], P('fsdp'), may hold values from -3 to 3
- expand_weight: bfloat16 [512, 2048], P('fsdp'), may hold values from -0.25 to 0.25
- expand_bias: bfloat16 [2048], P('fsdp'), may hold values from -3 to 3
- reduce_weight: bfloat16 [2048, 512], P('fsdp'), may hold values from -0.125 to 0.125
- reduce_bias: bfloat16 [512], P('fsdp'), may hold values from -3 to 3
Outputs:
- block_output: bfloat16 [256, 14, 14, 512], P(('fsdp', 'rep'))
- input_grad: float32 [256, 14, 14, 512], P(('fsdp', 'rep'))
- first_gain_grad: float32 [512], P('fsdp')
- first_shift_grad: float32 [512], P('fsdp')
- attend_weight_grad: float32 [512, 1536], P('fsdp')
- attend_bias_grad: float32 [1024], P('fsdp')
- bias_table_grad: float32 [169, 16], replicated
- output_weight_grad: float32 [512, 512], P('fsdp')
- output_bias_grad: float32 [512], P('fsdp')
- second_gain_grad: float32 [512], P('fsdp')
- second_shift_grad: float32 [512], P('fsdp')
- expand_weight_grad: float32 [512, 2048], P('fsdp')
- expand_bias_grad: float32 [2048], P('fsdp')
- reduce_weight_grad: float32 [2048, 512], P('fsdp')
- reduce_bias_grad: float32 [512], P('fsdp')
The draws below stay inside these ranges and needn't reach their ends.
Inputs may be any that keep to these rules, and one draw needn't show every extreme that they name: `image_counts`: in every draw one device holds 8 live images and another holds 1.
All inputs are finite; a program needn't handle non-finite values.
Results may differ from the reference program's by a relative error of at most 0.014.
Values may be sent and summed in bfloat16 or wider, within the bound.
No kernel may reach another device: no remote copies, remote signals or barrier semaphores. Data moves between devices by JAX's collectives and lax.ppermute only.
A program may use at most 192 MiB of HBM per device.

```python
import jax
import jax.numpy as jnp
from jax import lax

C = 512
HEADS = 16
HEAD_DIM = 32
MLP = 2048
WIN = 7
SHIFT = 3
IMG = 14
REGIONS = 4
IMG_CAP = 8
WINDOWS = 4
TOKW = 49
TABLE = 169
IMAGES = 256
N_FSDP = 8
N_REP = 4


def draw_image_counts(key, part):
    key = jax.random.fold_in(key, 7)
    count_key, full_key, least_key = jax.random.split(key, 3)
    devices_all = N_FSDP * N_REP
    counts = jax.random.randint(count_key, (devices_all,), 1, IMG_CAP + 1)
    fullest = jax.random.randint(full_key, (), 0, devices_all)
    step_away = jax.random.randint(least_key, (), 1, devices_all)
    emptiest = (fullest + step_away) % devices_all
    places = jnp.arange(devices_all)
    counts = jnp.where(places == fullest, IMG_CAP, counts)
    counts = jnp.where(places == emptiest, 1, counts)
    return counts.reshape(N_FSDP, N_REP).astype(jnp.int32)


def touch_ends(drawn, key, least, largest):
    longest = drawn.shape.index(max(drawn.shape))
    spots = []
    for shift in (0, 1):
        where = [jax.random.randint(jax.random.fold_in(key, axis), (), 0, length) for axis, length in enumerate(drawn.shape)]
        where[longest] = (where[longest] + shift) % drawn.shape[longest]
        spots.append(tuple(where))
    return drawn.at[spots[0]].set(least).at[spots[1]].set(largest)


def level_of(key, extent, cuts, low, largest):
    gain, own = 1.0, jax.random.fold_in(key, 6)
    for axis_at, shards_of in cuts:
        heights = jnp.exp(jax.random.uniform(jax.random.fold_in(own, axis_at), (shards_of,), jnp.float32, low / len(cuts), largest / len(cuts)))
        gain = gain * jnp.repeat(heights, extent[axis_at] // shards_of).reshape([-1 if axis == axis_at else 1 for axis in range(len(extent))])
    return gain


def noise(rng, extent, width, limit, pieces=(), kind=jnp.bfloat16):
    loudness = level_of(rng, extent, pieces, -0.22, 0.18) if pieces else 1.0
    drawn = jax.random.normal(rng, extent, jnp.float32) * width * loudness
    return jnp.minimum(jnp.maximum(drawn, -limit), limit).astype(kind)


def setup_inputs(seed: int = 0) -> dict:
    key_of = jax.random.split(jax.random.key(seed), 19)
    inputs = noise(key_of[0], (IMAGES, IMG, IMG, C), 1.0, 6.0, ((0, 32),))
    cotangent = noise(key_of[1], (IMAGES, IMG, IMG, C), 1.0, 6.0, ((0, 32),))
    image_counts = draw_image_counts(jax.random.fold_in(key_of[18], 71), 0)
    region_labels = touch_ends(jax.random.randint(key_of[3], (WINDOWS, TOKW), 0, REGIONS), jax.random.fold_in(key_of[3], 1), 0, REGIONS - 1).astype(jnp.int32)
    position_index = touch_ends(jax.random.randint(key_of[4], (TOKW, TOKW), 0, TABLE), jax.random.fold_in(key_of[4], 1), 0, TABLE - 1).astype(jnp.int32)
    first_gain = jnp.clip(1.0 + 0.15 * jax.random.normal(key_of[5], (C,), jnp.float32), 0.25, 1.75).astype(jnp.bfloat16)
    first_shift = noise(key_of[6], (C,), 0.3, 3.0, ((0, 8),))
    attend_weight = noise(key_of[7], (C, 3 * C), C ** -0.5, 0.25, ((0, 8),))
    attend_bias = noise(key_of[8], (2 * C,), 0.5, 3.0, ((0, 8),))
    bias_table = noise(key_of[9], (TABLE, HEADS), 1.0, 4.0)
    output_weight = noise(key_of[10], (C, C), (C // 12) ** -0.5, 1.0, ((0, 8),))
    output_bias = noise(key_of[11], (C,), 0.3, 3.0, ((0, 8),))
    second_gain = jnp.clip(1.0 + 0.15 * jax.random.normal(key_of[12], (C,), jnp.float32), 0.25, 1.75).astype(jnp.bfloat16)
    second_shift = noise(key_of[13], (C,), 0.3, 3.0, ((0, 8),))
    expand_weight = noise(key_of[14], (C, MLP), C ** -0.5, 0.25, ((0, 8),))
    expand_bias = noise(key_of[15], (MLP,), 0.5, 3.0, ((0, 8),))
    reduce_weight = noise(key_of[16], (MLP, C), MLP ** -0.5, 0.125, ((0, 8),))
    reduce_bias = noise(key_of[17], (C,), 0.3, 3.0, ((0, 8),))
    return {"inputs": inputs, "cotangent": cotangent, "image_counts": image_counts, "region_labels": region_labels, "position_index": position_index, "first_gain": first_gain, "first_shift": first_shift, "attend_weight": attend_weight, "attend_bias": attend_bias, "bias_table": bias_table, "output_weight": output_weight, "output_bias": output_bias, "second_gain": second_gain, "second_shift": second_shift, "expand_weight": expand_weight, "expand_bias": expand_bias, "reduce_weight": reduce_weight, "reduce_bias": reduce_bias}


@jax.custom_vjp
def low(v):
    return lax.optimization_barrier(v.astype(jnp.bfloat16)).astype(jnp.float32)

@jax.custom_vjp
def low_back(v):
    return v

def low_keep(v):
    return (low(v), None)

def low_pass(kept, grad):
    return (grad,)

def back_keep(v):
    return (v, None)

def back_low(kept, grad):
    return (low(grad),)
low.defvjp(low_keep, low_pass)
low_back.defvjp(back_keep, back_low)
epsilon = 1e-05
blocked = -1e+30
highest = lax.Precision.HIGHEST

def layer_norm(values, gain_vector, offset):
    centred = values - lax.optimization_barrier(jnp.mean(values, axis=-1, keepdims=True))
    inverse = lax.rsqrt(lax.optimization_barrier(jnp.mean(centred * centred, axis=-1, keepdims=True)) + epsilon)
    return centred * inverse * gain_vector + offset

def to_windows(grid_values):
    images = grid_values.shape[0]
    features = grid_values.shape[-1]
    rolled = jnp.roll(grid_values, (-SHIFT, -SHIFT), axis=(1, 2))
    parted = rolled.reshape(images, IMG // WIN, WIN, IMG // WIN, WIN, features)
    return parted.transpose(0, 1, 3, 2, 4, 5).reshape(images * WINDOWS, TOKW, features)

def from_windows(window_rows, images):
    features = window_rows.shape[-1]
    parted = window_rows.reshape(images, IMG // WIN, IMG // WIN, WIN, WIN, features).transpose(0, 1, 3, 2, 4, 5)
    return jnp.roll(parted.reshape(images, IMG, IMG, features), (SHIFT, SHIFT), axis=(1, 2))

def block_forward(params, grid_block, allowed, position_index):
    first_gain, first_shift, attend_weight, attend_bias, bias_table, output_weight, output_bias, second_gain, second_shift, expand_weight, expand_bias, reduce_weight, reduce_bias = params
    images = grid_block.shape[0]
    flat_rows = grid_block.reshape(images * IMG * IMG, C)
    attend_in = low(layer_norm(flat_rows, first_gain, first_shift))
    full_bias = jnp.concatenate([attend_bias[:C], jnp.zeros((C,), jnp.float32), attend_bias[C:]])
    packed = low(low_back(jnp.dot(attend_in, attend_weight, precision=highest) + full_bias))
    window_rows = to_windows(packed.reshape(images, IMG, IMG, 3 * C)).reshape(images, WINDOWS, TOKW, 3, HEADS, HEAD_DIM)
    queries = window_rows[:, :, :, 0]
    key_rows = window_rows[:, :, :, 1]
    value_rows = window_rows[:, :, :, 2]
    window_bias = jnp.transpose(bias_table[position_index], (2, 0, 1))
    raw_scores = jnp.einsum('bwqhd,bwkhd->bwhqk', queries, key_rows, precision=highest) * HEAD_DIM ** (-0.5) + window_bias
    scores = jnp.where(allowed[:, None], low_back(raw_scores), blocked)
    row_top = lax.optimization_barrier(jnp.max(scores, axis=-1, keepdims=True))
    exponent = jnp.exp(scores - row_top)
    softmax_weights = low(exponent / lax.optimization_barrier(jnp.sum(exponent, axis=-1, keepdims=True)))
    attended = jnp.einsum('bwhqk,bwkhd->bwqhd', softmax_weights, value_rows, precision=highest)
    attended = low(low_back(attended.reshape(images * WINDOWS, TOKW, C)))
    merged = from_windows(attended, images).reshape(images * IMG * IMG, C)
    residual = flat_rows + low_back(jnp.dot(merged, output_weight, precision=highest) + output_bias)
    expand_in = low(layer_norm(residual, second_gain, second_shift))
    pre_activation = low_back(jnp.dot(expand_in, expand_weight, precision=highest) + expand_bias)
    hidden = low(jax.nn.gelu(pre_activation, approximate=False))
    output_rows = residual + low_back(jnp.dot(hidden, reduce_weight, precision=highest) + reduce_bias)
    return output_rows.reshape(images, IMG, IMG, C)

def reference(inputs, cotangent, image_counts, region_labels, position_index, first_gain, first_shift, attend_weight, attend_bias, bias_table, output_weight, output_bias, second_gain, second_shift, expand_weight, expand_bias, reduce_weight, reduce_bias):
    params = tuple((member.astype(jnp.float32) for member in (first_gain, first_shift, attend_weight, attend_bias, bias_table, output_weight, output_bias, second_gain, second_shift, expand_weight, expand_bias, reduce_weight, reduce_bias)))
    groups = N_FSDP * N_REP
    live_images = (jnp.arange(IMG_CAP)[None, :] < image_counts.reshape(groups, 1)).astype(jnp.float32)
    grid_all = inputs.astype(jnp.float32).reshape(groups, IMG_CAP, IMG, IMG, C)
    cot_all = cotangent.astype(jnp.float32).reshape(groups, IMG_CAP, IMG, IMG, C)
    allowed = region_labels[:, :, None] == region_labels[:, None, :]

    def whole(weights, grid_values):

        def one_group(paired):
            rows = jax.checkpoint(block_forward)(weights, paired[0], allowed, position_index)
            return rows * paired[1][:, None, None, None]
        return lax.map(one_group, (grid_values, live_images))
    outputs, pullback = jax.vjp(whole, params, grid_all)
    weight_grads, input_grads = pullback(cot_all)
    return (outputs.astype(jnp.bfloat16).reshape(inputs.shape), input_grads.reshape(inputs.shape), weight_grads[0], weight_grads[1], weight_grads[2], weight_grads[3], weight_grads[4], weight_grads[5], weight_grads[6], weight_grads[7], weight_grads[8], weight_grads[9], weight_grads[10], weight_grads[11], weight_grads[12])
```

```python
import jax
import jax.numpy as jnp
import numpy as np
from jax import lax
from jax.experimental import pallas as pl
from jax.experimental.pallas import tpu as pltpu
from jax.sharding import PartitionSpec as P

C = 512
HEADS = 16
HEAD_DIM = 32
WIN = 7
SHIFT = 3
IMG = 14
WINDOWS = 4
TOKW = 49
TABLE = 169

TOK = IMG * IMG
ROWS = 208
RAW = 224
GROUP = 4
LANES = GROUP * HEAD_DIM
TABLE_PAD = 176

epsilon = 1e-05
blocked = -1e30
scale = HEAD_DIM ** (-0.5)
VMEM_BYTES = 56 * 1024 * 1024

F32 = jnp.float32
BF16 = jnp.bfloat16


def window_order():
    matrix = np.zeros((ROWS, RAW), np.float32)
    at = 0
    for wy in range(IMG // WIN):
        for wx in range(IMG // WIN):
            for ry in range(WIN):
                for rx in range(WIN):
                    gy = (wy * WIN + ry + SHIFT) % IMG
                    gx = (wx * WIN + rx + SHIFT) % IMG
                    matrix[at, 16 * gy + gx] = 1.0
                    at += 1
    return matrix


def dot(a, b):
    return jnp.dot(a, b, preferred_element_type=F32)


def dot_nt(a, b):
    return lax.dot_general(a, b, (((1,), (1,)), ((), ())), preferred_element_type=F32)


def turned(block):
    return block.astype(F32).T.astype(BF16)


def row_stats(values):
    centred = values - jnp.mean(values, axis=-1, keepdims=True)
    inverse = lax.rsqrt(jnp.mean(centred * centred, axis=-1, keepdims=True) + epsilon)
    return centred * inverse, inverse


def norm_pull(upstream, gain, unit, inverse):
    scaled = upstream * gain
    adjusted = (
        scaled
        - jnp.mean(scaled, axis=-1, keepdims=True)
        - unit * jnp.mean(scaled * unit, axis=-1, keepdims=True)
    )
    return adjusted * inverse


def column_sum(values):
    return jnp.sum(values, axis=0, keepdims=True)


def head_stack(block):
    lane = lax.broadcasted_iota(jnp.int32, block.shape, 1) // HEAD_DIM
    return jnp.concatenate(
        [jnp.where(lane == h, block, jnp.zeros_like(block)) for h in range(GROUP)], axis=0
    )


def head_pick(stacked):
    lane = lax.broadcasted_iota(jnp.int32, (ROWS, LANES), 1) // HEAD_DIM
    picked = stacked[:ROWS]
    for h in range(1, GROUP):
        picked = jnp.where(lane == h, stacked[h * ROWS : (h + 1) * ROWS], picked)
    return picked


def load_grid(grid_ref, rows_ref):
    @pl.when(pl.program_id(0) == 0)
    def _():
        rows_ref[...] = jnp.zeros_like(rows_ref)

    for r in range(IMG):
        rows_ref[16 * r : 16 * r + IMG, :] = grid_ref[0, r]


def bias_kernel(code_ref, codes_ref, index_ref, table_ref, out_ref):
    out_ref[...] = jnp.full(out_ref.shape, blocked, F32)
    entry = lax.broadcasted_iota(jnp.int32, (TABLE_PAD, ROWS), 0)
    codes = codes_ref[...]
    table = table_ref[...]
    for j in range(TOKW):
        hot = (entry == index_ref[j : j + 1, :]).astype(F32).astype(BF16)
        found = dot(table, hot)
        for w in range(WINDOWS):
            row = TOKW * w + j
            out_ref[:, row, :] = jnp.where(codes == code_ref[row], found, blocked)


def table_kernel(sums_ref, index_ref, out_ref):
    entry = lax.broadcasted_iota(jnp.int32, (TABLE_PAD, ROWS), 0)
    total = jnp.zeros((HEADS, TABLE_PAD), F32)
    for j in range(TOKW):
        part = sums_ref[:, j, :]
        for w in range(1, WINDOWS):
            part = part + sums_ref[:, TOKW * w + j, :]
        hot = (entry == index_ref[j : j + 1, :]).astype(F32).astype(BF16)
        high = part.astype(BF16)
        low = (part - high.astype(F32)).astype(BF16)
        total = total + dot_nt(high, hot) + dot_nt(low, hot)
    out_ref[...] = total


def attend_kernel(
    grid_ref, order_ref, gain_ref, shift_ref, weight_ref, bias_ref, pair_ref,
    win_ref, in_ref, packed_ref, soft_ref, merged_ref, rows_ref,
):
    load_grid(grid_ref, rows_ref)
    values = dot(order_ref[...], rows_ref[...])
    win_ref[...] = values.astype(BF16)
    unit, _ = row_stats(values)
    attend_in = (unit * gain_ref[...] + shift_ref[...]).astype(BF16)
    in_ref[...] = attend_in
    packed_ref[...] = (dot(attend_in, weight_ref[...]) + bias_ref[...]).astype(BF16)
    for g in range(HEADS // GROUP):
        at = LANES * g
        q = packed_ref[:, at : at + LANES]
        k = packed_ref[:, C + at : C + at + LANES]
        v_turned = turned(packed_ref[:, 2 * C + at : 2 * C + at + LANES])
        raw = dot_nt(head_stack(k), q)
        parts = []
        for h in range(GROUP):
            s = raw[h * ROWS : (h + 1) * ROWS] * scale + pair_ref[g * GROUP + h]
            e = jnp.exp(s - jnp.max(s, axis=0, keepdims=True))
            p = (e * (1.0 / column_sum(e))).astype(BF16)
            soft_ref[0, g * GROUP + h] = p
            parts.append(dot(v_turned[h * HEAD_DIM : (h + 1) * HEAD_DIM], p))
        merged_ref[:, at : at + LANES] = jnp.concatenate(parts, axis=0).T.astype(BF16)


def mlp_kernel(
    count_ref, win_ref, merged_ref, grid_ref, order_ref, back_ref, out_w_ref, out_b_ref,
    gain_ref, shift_ref, exp_w_ref, exp_b_ref, red_w_ref, red_b_ref,
    block_ref, hidden_ref, d_pre_ref, in_ref, grad_ref, d_res_ref, d_branch_ref, d_att_ref,
    sums_ref, wide_ref, rows_ref,
):
    image = pl.program_id(0)

    @pl.when(image == 0)
    def _():
        sums_ref[...] = jnp.zeros_like(sums_ref)
        wide_ref[...] = jnp.zeros_like(wide_ref)

    live = (image < count_ref[0]).astype(F32)
    load_grid(grid_ref, rows_ref)
    grad = dot(order_ref[...], rows_ref[...]) * live
    grad_low = grad.astype(BF16)
    grad_ref[...] = grad_low
    residual = win_ref[...].astype(F32) + dot(merged_ref[...], out_w_ref[...]) + out_b_ref[...]
    unit, inverse = row_stats(residual)
    expand_in = (unit * gain_ref[...] + shift_ref[...]).astype(BF16)
    in_ref[...] = expand_in
    mlp = exp_w_ref.shape[1]
    step = 512
    out = residual + red_b_ref[...]
    d_in = jnp.zeros((ROWS, C), F32)
    for m in range(0, mlp, step):
        cols = slice(m, m + step)
        pre = dot(expand_in, exp_w_ref[:, cols]) + exp_b_ref[:, cols]
        bell = jnp.exp(pre * pre * -0.5)
        t = 1.0 / (1.0 + jnp.abs(pre) * (0.3275911 * 0.7071067811865476))
        tail = (
            t
            * bell
            * (
                0.127414796
                + t * (-0.142248368 + t * (0.7107068705 + t * (-0.7265760135 + t * 0.5307027145)))
            )
        )
        cdf = jnp.where(pre >= 0, 1.0 - tail, tail)
        hidden = (pre * cdf).astype(BF16)
        hidden_ref[:, cols] = hidden
        d_hidden = dot_nt(grad_low, red_w_ref[cols, :])
        d_pre = (d_hidden * (cdf + pre * bell * 0.3989422804014327)).astype(BF16)
        d_pre_ref[:, cols] = d_pre
        wide_ref[:, cols] += column_sum(d_pre.astype(F32))
        out = out + dot(hidden, red_w_ref[cols, :])
        d_in = d_in + dot_nt(d_pre, exp_w_ref[:, cols])
    block = (out * live).astype(BF16)
    block_rows = dot(back_ref[...], block).astype(BF16)
    for r in range(IMG):
        block_ref[0, r] = block_rows[16 * r : 16 * r + IMG]
    d_res = grad + norm_pull(d_in, gain_ref[...], unit, inverse)
    d_res_ref[...] = d_res
    d_branch = d_res.astype(BF16)
    d_branch_ref[...] = d_branch
    d_att_ref[...] = dot_nt(d_branch, out_w_ref[...]).astype(BF16)
    sums_ref[0:1, :] += column_sum(d_in * unit)
    sums_ref[1:2, :] += column_sum(d_in)
    sums_ref[2:3, :] += column_sum(d_branch.astype(F32))
    sums_ref[3:4, :] += column_sum(grad)


def attend_back_kernel(packed_ref, soft_ref, d_att_ref, d_packed_ref, pairs_ref):
    @pl.when(pl.program_id(0) == 0)
    def _():
        pairs_ref[...] = jnp.zeros_like(pairs_ref)

    for g in range(HEADS // GROUP):
        at = LANES * g
        q = packed_ref[:, at : at + LANES]
        k_turned = turned(packed_ref[:, C + at : C + at + LANES])
        v = packed_ref[:, 2 * C + at : 2 * C + at + LANES]
        d_att = d_att_ref[:, at : at + LANES]
        d_soft = dot_nt(head_stack(v), d_att)
        d_raw, d_q, soft = [], [], []
        for h in range(GROUP):
            head = g * GROUP + h
            low = soft_ref[0, head]
            soft.append(low)
            p = low.astype(F32)
            dp = d_soft[h * ROWS : (h + 1) * ROWS]
            ds = (p * (dp - column_sum(p * dp))).astype(BF16)
            pairs_ref[head] += ds.astype(F32)
            d_raw.append(ds)
            d_q.append(dot(k_turned[h * HEAD_DIM : (h + 1) * HEAD_DIM], ds))
        d_k = head_pick(dot(jnp.concatenate(d_raw, axis=0), q))
        d_v = head_pick(dot(jnp.concatenate(soft, axis=0), d_att))
        d_packed_ref[:, at : at + LANES] = (jnp.concatenate(d_q, axis=0) * scale).T.astype(BF16)
        d_packed_ref[:, C + at : C + at + LANES] = (d_k * scale).astype(BF16)
        d_packed_ref[:, 2 * C + at : 2 * C + at + LANES] = d_v.astype(BF16)


def input_kernel(
    d_packed_ref, win_ref, d_res_ref, gain_ref, weight_ref, back_ref,
    grad_ref, sums_ref, wide_ref,
):
    @pl.when(pl.program_id(0) == 0)
    def _():
        sums_ref[...] = jnp.zeros_like(sums_ref)
        wide_ref[...] = jnp.zeros_like(wide_ref)

    d_packed = d_packed_ref[...]
    d_in = dot_nt(d_packed, weight_ref[...])
    unit, inverse = row_stats(win_ref[...].astype(F32))
    total = d_res_ref[...] + norm_pull(d_in, gain_ref[...], unit, inverse)
    sums_ref[0:1, :] += column_sum(d_in * unit)
    sums_ref[1:2, :] += column_sum(d_in)
    wide_ref[...] += column_sum(d_packed.astype(F32))
    high = total.astype(BF16)
    low = (total - high.astype(F32)).astype(BF16)
    rows = dot(back_ref[...], high) + dot(back_ref[...], low)
    for r in range(IMG):
        grad_ref[0, r] = rows[16 * r : 16 * r + IMG]


def whole(shape):
    return pl.BlockSpec(shape, lambda *_: (0,) * len(shape))


def per_image(width):
    return pl.BlockSpec((ROWS, width), lambda i: (i, 0))


GRID_SPEC = pl.BlockSpec((1, IMG, IMG, C), lambda i: (i, 0, 0, 0))
SMEM_SPEC = pl.BlockSpec(memory_space=pltpu.SMEM)


def params():
    return pltpu.CompilerParams(vmem_limit_bytes=VMEM_BYTES)


def cost(flops, moved, special=0):
    return pl.CostEstimate(flops=int(flops), bytes_accessed=int(moved), transcendentals=int(special))


def struct(shape, dtype):
    return jax.ShapeDtypeStruct(shape, dtype)


def run_bias(codes, index_rows, table):
    return pl.pallas_call(
        bias_kernel,
        out_shape=struct((HEADS, ROWS, ROWS), F32),
        in_specs=[SMEM_SPEC] + [pl.BlockSpec(memory_space=pltpu.VMEM)] * 3,
        out_specs=pl.BlockSpec(memory_space=pltpu.VMEM),
        compiler_params=params(),
        cost_estimate=cost(2e9, 4e6),
    )(codes, codes[None, :], index_rows, table)


def run_table(pairs, index_rows):
    return pl.pallas_call(
        table_kernel,
        out_shape=struct((HEADS, TABLE_PAD), F32),
        in_specs=[pl.BlockSpec(memory_space=pltpu.VMEM)] * 2,
        out_specs=pl.BlockSpec(memory_space=pltpu.VMEM),
        compiler_params=params(),
        cost_estimate=cost(2e9, 4e6),
    )(pairs, index_rows)


def run_attend(inputs, order, gain, shift, weight, bias, pair):
    images = inputs.shape[0]
    rows = images * ROWS
    return pl.pallas_call(
        attend_kernel,
        grid=(images,),
        out_shape=(
            struct((rows, C), BF16),
            struct((rows, C), BF16),
            struct((rows, 3 * C), BF16),
            struct((images, HEADS, ROWS, ROWS), BF16),
            struct((rows, C), BF16),
        ),
        in_specs=[
            GRID_SPEC,
            whole((ROWS, RAW)),
            whole((1, C)),
            whole((1, C)),
            whole((C, 3 * C)),
            whole((1, 3 * C)),
            whole((HEADS, ROWS, ROWS)),
        ],
        out_specs=(
            per_image(C),
            per_image(C),
            per_image(3 * C),
            pl.BlockSpec((1, HEADS, ROWS, ROWS), lambda i: (i, 0, 0, 0)),
            per_image(C),
        ),
        scratch_shapes=[pltpu.VMEM((RAW, C), BF16)],
        compiler_params=params(),
        cost_estimate=cost(images * 5e9, images * 6e6),
    )(inputs, order, gain, shift, weight, bias, pair)


def run_mlp(count, win, merged, cotangent, order, back, weights):
    images = cotangent.shape[0]
    rows = images * ROWS
    mlp = weights[4].shape[1]
    return pl.pallas_call(
        mlp_kernel,
        grid=(images,),
        out_shape=(
            struct(cotangent.shape, BF16),
            struct((rows, mlp), BF16),
            struct((rows, mlp), BF16),
            struct((rows, C), BF16),
            struct((rows, C), BF16),
            struct((rows, C), F32),
            struct((rows, C), BF16),
            struct((rows, C), BF16),
            struct((8, C), F32),
            struct((1, mlp), F32),
        ),
        in_specs=[
            SMEM_SPEC,
            per_image(C),
            per_image(C),
            GRID_SPEC,
            whole((ROWS, RAW)),
            whole((RAW, ROWS)),
            whole((C, C)),
            whole((1, C)),
            whole((1, C)),
            whole((1, C)),
            whole((C, mlp)),
            whole((1, mlp)),
            whole((mlp, C)),
            whole((1, C)),
        ],
        out_specs=(
            GRID_SPEC,
            per_image(mlp),
            per_image(mlp),
            per_image(C),
            per_image(C),
            per_image(C),
            per_image(C),
            per_image(C),
            whole((8, C)),
            whole((1, mlp)),
        ),
        scratch_shapes=[pltpu.VMEM((RAW, C), BF16)],
        compiler_params=params(),
        cost_estimate=cost(images * 6e9, images * 4e6),
    )(count, win, merged, cotangent, order, back, *weights)


def run_attend_back(packed, soft, d_att):
    images = soft.shape[0]
    return pl.pallas_call(
        attend_back_kernel,
        grid=(images,),
        out_shape=(struct(packed.shape, BF16), struct((HEADS, ROWS, ROWS), F32)),
        in_specs=[
            per_image(3 * C),
            pl.BlockSpec((1, HEADS, ROWS, ROWS), lambda i: (i, 0, 0, 0)),
            per_image(C),
        ],
        out_specs=(per_image(3 * C), whole((HEADS, ROWS, ROWS))),
        compiler_params=params(),
        cost_estimate=cost(images * 6e9, images * 6e6),
    )(packed, soft, d_att)


def run_input(d_packed, win, d_res, gain, weight, back, shape):
    return pl.pallas_call(
        input_kernel,
        grid=(shape[0],),
        out_shape=(struct(shape, F32), struct((8, C), F32), struct((1, 3 * C), F32)),
        in_specs=[
            per_image(3 * C),
            per_image(C),
            per_image(C),
            whole((1, C)),
            whole((C, 3 * C)),
            whole((RAW, ROWS)),
        ],
        out_specs=(GRID_SPEC, whole((8, C)), whole((1, 3 * C))),
        compiler_params=params(),
        cost_estimate=cost(shape[0] * 1e9, shape[0] * 2e6),
    )(d_packed, win, d_res, gain, weight, back)


def weight_grad(rows_in, rows_out):
    return lax.dot_general(
        rows_in, rows_out, (((0,), (0,)), ((), ())), preferred_element_type=F32
    ).astype(BF16)


def gather(shard):
    return lax.all_gather(shard, "fsdp", axis=0, tiled=True)


def reduce_weight_grad(partial):
    share = lax.psum_scatter(partial, "fsdp", scatter_dimension=0, tiled=True)
    return lax.psum(share, "rep").astype(F32)


def per_device(
    inputs,
    cotangent,
    image_counts,
    region_labels,
    position_index,
    first_gain,
    first_shift,
    attend_weight,
    attend_bias,
    bias_table,
    output_weight,
    output_bias,
    second_gain,
    second_shift,
    expand_weight,
    expand_bias,
    reduce_weight,
    reduce_bias,
):
    order_host = window_order()
    order = jnp.asarray(order_host, BF16)
    back = jnp.asarray(order_host.T, BF16)
    shards = lax.axis_size("fsdp")
    mine = lax.axis_index("fsdp")

    window_of = jnp.arange(WINDOWS, dtype=jnp.int32)[:, None]
    codes = jnp.pad(
        (region_labels + 4 * window_of).reshape(-1), (0, ROWS - TOK), constant_values=-1
    )
    index_rows = jnp.pad(jnp.tile(position_index.T, (1, WINDOWS)), ((0, 0), (0, ROWS - TOK)))
    table = jnp.pad(bias_table.T, ((0, 0), (0, TABLE_PAD - TABLE)))
    pair = run_bias(codes, index_rows, table)

    vectors = (
        first_gain, first_shift, attend_bias, output_bias,
        second_gain, second_shift, expand_bias, reduce_bias,
    )
    sizes = [v.shape[0] for v in vectors]
    joined = gather(jnp.concatenate(vectors)).reshape(shards, sum(sizes)).astype(F32)
    cuts = np.cumsum([0] + sizes)
    full = [
        joined[:, cuts[i] : cuts[i + 1]].reshape(1, shards * sizes[i]) for i in range(len(sizes))
    ]
    gain_one, shift_one, bias_one, bias_out, gain_two, shift_two, bias_exp, bias_red = full
    bias_packed = jnp.concatenate(
        [bias_one[:, :C], jnp.zeros((1, C), F32), bias_one[:, C:]], axis=1
    )
    weight_one = gather(attend_weight)
    weight_out = gather(output_weight)
    weight_exp = gather(expand_weight)
    weight_red = gather(reduce_weight)

    win, attend_in, packed, soft, merged = run_attend(
        inputs, order, gain_one, shift_one, weight_one, bias_packed, pair
    )
    (
        block_output, hidden, d_pre, expand_in, grad_low, d_res, d_branch, d_att, sums_two, d_exp_bias,
    ) = run_mlp(
        image_counts.reshape(1), win, merged, cotangent, order, back,
        (weight_out, bias_out, gain_two, shift_two, weight_exp, bias_exp, weight_red, bias_red),
    )
    reduce_grad = reduce_weight_grad(weight_grad(hidden, grad_low))
    expand_grad = reduce_weight_grad(weight_grad(expand_in, d_pre))
    output_grad = reduce_weight_grad(weight_grad(merged, d_branch))
    d_packed, pairs = run_attend_back(packed, soft, d_att)
    attend_grad = reduce_weight_grad(weight_grad(attend_in, d_packed))
    input_grad, sums_one, d_packed_bias = run_input(
        d_packed, win, d_res, gain_one, weight_one, back, inputs.shape
    )
    table_part = run_table(pairs, index_rows)
    small = (
        sums_one[0], sums_one[1], d_packed_bias[0, :C], d_packed_bias[0, 2 * C :],
        sums_two[2], sums_two[0], sums_two[1], d_exp_bias[0], sums_two[3], table_part.reshape(-1),
    )
    small_sizes = np.cumsum([0] + [s.shape[0] for s in small])
    summed = lax.psum(jnp.concatenate(small), ("fsdp", "rep"))
    parts = [summed[small_sizes[i] : small_sizes[i + 1]] for i in range(len(small))]
    parts = parts[:2] + [jnp.concatenate(parts[2:4])] + parts[4:]

    def own(vector):
        size = vector.shape[0] // shards
        return lax.dynamic_slice(vector, (mine * size,), (size,))

    table_grad = parts[8].reshape(HEADS, TABLE_PAD)[:, :TABLE].T
    return (
        block_output,
        input_grad,
        own(parts[0]),
        own(parts[1]),
        attend_grad,
        own(parts[2]),
        table_grad,
        output_grad,
        own(parts[3]),
        own(parts[4]),
        own(parts[5]),
        expand_grad,
        own(parts[6]),
        reduce_grad,
        own(parts[7]),
    )


def solution(mesh):
    images = P(("fsdp", "rep"), None, None, None)
    rows, vector = P("fsdp", None), P("fsdp")
    return jax.shard_map(
        per_device,
        mesh=mesh,
        in_specs=(
            images, images, P("fsdp", "rep"), P(), P(), vector, vector, rows, vector, P(),
            rows, vector, vector, vector, rows, vector, rows, vector,
        ),
        out_specs=(
            images, images, vector, vector, rows, vector, P(), rows, vector, vector, vector,
            rows, vector, rows, vector,
        ),
        check_vma=False,
    )
```

```python
import jax
import jax.numpy as jnp
import numpy as np
from jax import lax
from jax.experimental import pallas as pl
from jax.experimental.pallas import tpu as pltpu
from jax.sharding import PartitionSpec as P

C = 512
HEADS = 16
HEAD_DIM = 32
WIN = 7
SHIFT = 3
IMG = 14
WINDOWS = 4
TOKW = 49
TABLE = 169

TOK = IMG * IMG
ROWS = 208
RAW = 224
GROUP = 4
LANES = GROUP * HEAD_DIM
TABLE_PAD = 176

epsilon = 1e-05
blocked = -1e30
scale = HEAD_DIM ** (-0.5)
VMEM_BYTES = 56 * 1024 * 1024

F32 = jnp.float32
BF16 = jnp.bfloat16


def window_order():
    matrix = np.zeros((ROWS, RAW), np.float32)
    at = 0
    for wy in range(IMG // WIN):
        for wx in range(IMG // WIN):
            for ry in range(WIN):
                for rx in range(WIN):
                    gy = (wy * WIN + ry + SHIFT) % IMG
                    gx = (wx * WIN + rx + SHIFT) % IMG
                    matrix[at, 16 * gy + gx] = 1.0
                    at += 1
    return matrix


def dot(a, b):
    return jnp.dot(a, b, preferred_element_type=F32)


def dot_nt(a, b):
    return lax.dot_general(a, b, (((1,), (1,)), ((), ())), preferred_element_type=F32)


def turned(block):
    return block.astype(F32).T.astype(BF16)


def row_stats(values):
    centred = values - jnp.mean(values, axis=-1, keepdims=True)
    inverse = lax.rsqrt(jnp.mean(centred * centred, axis=-1, keepdims=True) + epsilon)
    return centred * inverse, inverse


def norm_pull(upstream, gain, unit, inverse):
    scaled = upstream * gain
    adjusted = (
        scaled
        - jnp.mean(scaled, axis=-1, keepdims=True)
        - unit * jnp.mean(scaled * unit, axis=-1, keepdims=True)
    )
    return adjusted * inverse


def column_sum(values):
    return jnp.sum(values, axis=0, keepdims=True)


def head_stack(block):
    lane = lax.broadcasted_iota(jnp.int32, block.shape, 1) // HEAD_DIM
    return jnp.concatenate(
        [jnp.where(lane == h, block, jnp.zeros_like(block)) for h in range(GROUP)], axis=0
    )


def head_pick(stacked):
    lane = lax.broadcasted_iota(jnp.int32, (ROWS, LANES), 1) // HEAD_DIM
    picked = stacked[:ROWS]
    for h in range(1, GROUP):
        picked = jnp.where(lane == h, stacked[h * ROWS : (h + 1) * ROWS], picked)
    return picked


def load_grid(grid_ref, rows_ref):
    @pl.when(pl.program_id(0) == 0)
    def _():
        rows_ref[...] = jnp.zeros_like(rows_ref)

    for r in range(IMG):
        rows_ref[16 * r : 16 * r + IMG, :] = grid_ref[0, r]


def bias_kernel(code_ref, codes_ref, index_ref, table_ref, out_ref):
    out_ref[...] = jnp.full(out_ref.shape, blocked, F32)
    entry = lax.broadcasted_iota(jnp.int32, (TABLE_PAD, ROWS), 0)
    codes = codes_ref[...]
    table = table_ref[...]
    for j in range(TOKW):
        hot = (entry == index_ref[j : j + 1, :]).astype(F32).astype(BF16)
        found = dot(table, hot)
        for w in range(WINDOWS):
            row = TOKW * w + j
            out_ref[:, row, :] = jnp.where(codes == code_ref[row], found, blocked)


def table_kernel(sums_ref, index_ref, out_ref, window_ref):
    for h in range(HEADS):
        part = sums_ref[h, :TOKW, :]
        for w in range(1, WINDOWS):
            part = part + sums_ref[h, TOKW * w : TOKW * (w + 1), :]
        window_ref[h, :TOKW, :] = part
    entry = lax.broadcasted_iota(jnp.int32, (TABLE_PAD, ROWS), 0)
    total = jnp.zeros((2 * HEADS, TABLE_PAD), F32)
    for j in range(TOKW):
        part = window_ref[:, j, :]
        hot = (entry == index_ref[j : j + 1, :]).astype(F32).astype(BF16)
        high = part.astype(BF16)
        low = (part - high.astype(F32)).astype(BF16)
        total = total + dot_nt(jnp.concatenate([high, low], axis=0), hot)
    out_ref[...] = total[:HEADS] + total[HEADS:]


def attend_kernel(starts_ref, grid_ref, order_ref, gain_ref, shift_ref, bias_ref, pair_ref, *rest):
    pieces = rest[:-7]
    win_ref, in_ref, packed_ref, soft_ref, merged_ref, weight_ref, rows_ref = rest[-7:]

    @pl.when(pl.program_id(0) == 0)
    def _():
        rows = weight_ref.shape[0] // starts_ref.shape[0]
        at = 0
        for piece in pieces:
            for r in range(0, piece.shape[0], rows):
                start = pl.multiple_of(starts_ref[at], rows)
                weight_ref[pl.ds(start, rows), :] = piece[r : r + rows, :]
                at += 1

    load_grid(grid_ref, rows_ref)
    values = dot(order_ref[...], rows_ref[...])
    win_ref[...] = values.astype(BF16)
    unit, _ = row_stats(values)
    attend_in = (unit * gain_ref[...] + shift_ref[...]).astype(BF16)
    in_ref[...] = attend_in
    packed_ref[...] = (dot(attend_in, weight_ref[...]) + bias_ref[...]).astype(BF16)
    for g in range(HEADS // GROUP):
        at = LANES * g
        q = packed_ref[:, at : at + LANES]
        k = packed_ref[:, C + at : C + at + LANES]
        v_turned = turned(packed_ref[:, 2 * C + at : 2 * C + at + LANES])
        raw = dot_nt(head_stack(k), q)
        parts = []
        for h in range(GROUP):
            s = raw[h * ROWS : (h + 1) * ROWS] * scale + pair_ref[g * GROUP + h]
            e = jnp.exp(s - jnp.max(s, axis=0, keepdims=True))
            p = (e * (1.0 / column_sum(e))).astype(BF16)
            soft_ref[0, g * GROUP + h] = p
            parts.append(dot(v_turned[h * HEAD_DIM : (h + 1) * HEAD_DIM], p))
        merged_ref[:, at : at + LANES] = jnp.concatenate(parts, axis=0).T.astype(BF16)


def mlp_kernel(
    count_ref, win_ref, merged_ref, grid_ref, order_ref, back_ref, out_b_ref,
    gain_ref, shift_ref, exp_b_ref, red_b_ref, joined_ref,
    block_ref, hidden_ref, d_pre_ref, in_ref, grad_ref, d_res_ref, d_branch_ref, d_att_ref,
    sums_ref, wide_ref, rows_ref, red_w_ref, red_t_ref, exp_t_ref, out_t_ref,
):
    image = pl.program_id(0)
    mlp = exp_b_ref.shape[1]
    blocks = mlp // C
    out_w_ref = joined_ref.at[:, :C]
    exp_w_ref = joined_ref.at[:, C : C + mlp]

    @pl.when(image == 0)
    def _():
        sums_ref[...] = jnp.zeros_like(sums_ref)
        wide_ref[...] = jnp.zeros_like(wide_ref)
        for at in range(0, C, 16):
            for b in range(blocks):
                cols = C + mlp + b * C
                red_w_ref[blocks * at + 16 * b : blocks * at + 16 * (b + 1), :] = joined_ref[
                    at : at + 16, cols : cols + C
                ]
        out_t_ref[...] = turned(out_w_ref[...])
        for m in range(0, mlp, C):
            red_t_ref[:, m : m + C] = turned(red_w_ref[m : m + C, :])
            exp_t_ref[m : m + C, :] = turned(exp_w_ref[:, m : m + C])

    live = (image < count_ref[0]).astype(F32)
    load_grid(grid_ref, rows_ref)
    grad = dot(order_ref[...], rows_ref[...]) * live
    grad_low = grad.astype(BF16)
    grad_ref[...] = grad_low
    residual = win_ref[...].astype(F32) + dot(merged_ref[...], out_w_ref[...]) + out_b_ref[...]
    unit, inverse = row_stats(residual)
    expand_in = (unit * gain_ref[...] + shift_ref[...]).astype(BF16)
    in_ref[...] = expand_in
    step = 512
    out = residual + red_b_ref[...]
    d_in = jnp.zeros((ROWS, C), F32)
    for m in range(0, mlp, step):
        cols = slice(m, m + step)
        pre = dot(expand_in, exp_w_ref[:, cols]) + exp_b_ref[:, cols]
        bell = jnp.exp(pre * pre * -0.5)
        t = 1.0 / (1.0 + jnp.abs(pre) * (0.3275911 * 0.7071067811865476))
        tail = (
            t
            * bell
            * (
                0.127414796
                + t * (-0.142248368 + t * (0.7107068705 + t * (-0.7265760135 + t * 0.5307027145)))
            )
        )
        cdf = jnp.where(pre >= 0, 1.0 - tail, tail)
        hidden = (pre * cdf).astype(BF16)
        hidden_ref[:, cols] = hidden
        d_hidden = dot(grad_low, red_t_ref[:, cols])
        d_pre = (d_hidden * (cdf + pre * bell * 0.3989422804014327)).astype(BF16)
        d_pre_ref[:, cols] = d_pre
        wide_ref[:, cols] += column_sum(d_pre.astype(F32))
        out = out + dot(hidden, red_w_ref[cols, :])
        d_in = d_in + dot(d_pre, exp_t_ref[cols, :])
    block = (out * live).astype(BF16)
    block_rows = dot(back_ref[...], block).astype(BF16)
    for r in range(IMG):
        block_ref[0, r] = block_rows[16 * r : 16 * r + IMG]
    d_res = grad + norm_pull(d_in, gain_ref[...], unit, inverse)
    d_res_ref[...] = d_res
    d_branch = d_res.astype(BF16)
    d_branch_ref[...] = d_branch
    d_att_ref[...] = dot(d_branch, out_t_ref[...]).astype(BF16)
    sums_ref[0:1, :] += column_sum(d_in * unit)
    sums_ref[1:2, :] += column_sum(d_in)
    sums_ref[2:3, :] += column_sum(d_branch.astype(F32))
    sums_ref[3:4, :] += column_sum(grad)


def attend_back_kernel(packed_ref, soft_ref, d_att_ref, d_packed_ref, pairs_ref):
    @pl.when(pl.program_id(0) == 0)
    def _():
        pairs_ref[...] = jnp.zeros_like(pairs_ref)

    for g in range(HEADS // GROUP):
        at = LANES * g
        q = packed_ref[:, at : at + LANES]
        k_turned = turned(packed_ref[:, C + at : C + at + LANES])
        v = packed_ref[:, 2 * C + at : 2 * C + at + LANES]
        d_att = d_att_ref[:, at : at + LANES]
        d_soft = dot_nt(head_stack(v), d_att)
        d_raw, d_q, soft = [], [], []
        for h in range(GROUP):
            head = g * GROUP + h
            low = soft_ref[0, head]
            soft.append(low)
            p = low.astype(F32)
            dp = d_soft[h * ROWS : (h + 1) * ROWS]
            ds = (p * (dp - column_sum(p * dp))).astype(BF16)
            pairs_ref[head] += ds.astype(F32)
            d_raw.append(ds)
            d_q.append(dot(k_turned[h * HEAD_DIM : (h + 1) * HEAD_DIM], ds))
        d_k = head_pick(dot(jnp.concatenate(d_raw, axis=0), q))
        d_v = head_pick(dot(jnp.concatenate(soft, axis=0), d_att))
        d_packed_ref[:, at : at + LANES] = (jnp.concatenate(d_q, axis=0) * scale).T.astype(BF16)
        d_packed_ref[:, C + at : C + at + LANES] = (d_k * scale).astype(BF16)
        d_packed_ref[:, 2 * C + at : 2 * C + at + LANES] = d_v.astype(BF16)


def input_kernel(
    d_packed_ref, win_ref, d_res_ref, gain_ref, weight_ref, back_ref,
    grad_ref, sums_ref, wide_ref, turned_ref,
):
    @pl.when(pl.program_id(0) == 0)
    def _():
        for m in range(0, 3 * C, C):
            turned_ref[m : m + C, :] = turned(weight_ref[:, m : m + C])
        sums_ref[...] = jnp.zeros_like(sums_ref)
        wide_ref[...] = jnp.zeros_like(wide_ref)

    d_packed = d_packed_ref[...]
    d_in = dot(d_packed, turned_ref[...])
    unit, inverse = row_stats(win_ref[...].astype(F32))
    total = d_res_ref[...] + norm_pull(d_in, gain_ref[...], unit, inverse)
    sums_ref[0:1, :] += column_sum(d_in * unit)
    sums_ref[1:2, :] += column_sum(d_in)
    wide_ref[...] += column_sum(d_packed.astype(F32))
    high = total.astype(BF16)
    low = (total - high.astype(F32)).astype(BF16)
    rows = dot(back_ref[...], high) + dot(back_ref[...], low)
    for r in range(IMG):
        grad_ref[0, r] = rows[16 * r : 16 * r + IMG]


def whole(shape):
    return pl.BlockSpec(shape, lambda *_: (0,) * len(shape))


def per_image(width):
    return pl.BlockSpec((ROWS, width), lambda i: (i, 0))


GRID_SPEC = pl.BlockSpec((1, IMG, IMG, C), lambda i: (i, 0, 0, 0))
SMEM_SPEC = pl.BlockSpec(memory_space=pltpu.SMEM)


def params():
    return pltpu.CompilerParams(vmem_limit_bytes=VMEM_BYTES)


def cost(flops, moved, special=0):
    return pl.CostEstimate(flops=int(flops), bytes_accessed=int(moved), transcendentals=int(special))


def struct(shape, dtype):
    return jax.ShapeDtypeStruct(shape, dtype)


def run_bias(codes, index_rows, table):
    return pl.pallas_call(
        bias_kernel,
        out_shape=struct((HEADS, ROWS, ROWS), F32),
        in_specs=[SMEM_SPEC] + [pl.BlockSpec(memory_space=pltpu.VMEM)] * 3,
        out_specs=pl.BlockSpec(memory_space=pltpu.VMEM),
        compiler_params=params(),
        cost_estimate=cost(2e9, 4e6),
    )(codes, codes[None, :], index_rows, table)


def run_table(pairs, index_rows):
    return pl.pallas_call(
        table_kernel,
        out_shape=struct((HEADS, TABLE_PAD), F32),
        in_specs=[pl.BlockSpec(memory_space=pltpu.VMEM)] * 2,
        out_specs=pl.BlockSpec(memory_space=pltpu.VMEM),
        scratch_shapes=[pltpu.VMEM((HEADS, 56, ROWS), F32)],
        compiler_params=params(),
        cost_estimate=cost(2e9, 4e6),
    )(pairs, index_rows)


def run_attend(inputs, order, gain, shift, starts, pieces, bias, pair):
    images = inputs.shape[0]
    rows = images * ROWS
    return pl.pallas_call(
        attend_kernel,
        grid=(images,),
        out_shape=(
            struct((rows, C), BF16),
            struct((rows, C), BF16),
            struct((rows, 3 * C), BF16),
            struct((images, HEADS, ROWS, ROWS), BF16),
            struct((rows, C), BF16),
            struct((C, 3 * C), BF16),
        ),
        in_specs=[
            SMEM_SPEC,
            GRID_SPEC,
            whole((ROWS, RAW)),
            whole((1, C)),
            whole((1, C)),
            whole((1, 3 * C)),
            whole((HEADS, ROWS, ROWS)),
        ]
        + [whole(piece.shape) for piece in pieces],
        out_specs=(
            per_image(C),
            per_image(C),
            per_image(3 * C),
            pl.BlockSpec((1, HEADS, ROWS, ROWS), lambda i: (i, 0, 0, 0)),
            per_image(C),
            whole((C, 3 * C)),
        ),
        scratch_shapes=[pltpu.VMEM((RAW, C), BF16)],
        compiler_params=params(),
        cost_estimate=cost(images * 5e9, images * 6e6),
    )(starts, inputs, order, gain, shift, bias, pair, *pieces)


def run_mlp(count, win, merged, cotangent, order, back, weights):
    images = cotangent.shape[0]
    rows = images * ROWS
    mlp = weights[3].shape[1]
    return pl.pallas_call(
        mlp_kernel,
        grid=(images,),
        out_shape=(
            struct(cotangent.shape, BF16),
            struct((rows, mlp), BF16),
            struct((rows, mlp), BF16),
            struct((rows, C), BF16),
            struct((rows, C), BF16),
            struct((rows, C), F32),
            struct((rows, C), BF16),
            struct((rows, C), BF16),
            struct((8, C), F32),
            struct((1, mlp), F32),
        ),
        in_specs=[
            SMEM_SPEC,
            per_image(C),
            per_image(C),
            GRID_SPEC,
            whole((ROWS, RAW)),
            whole((RAW, ROWS)),
            whole((1, C)),
            whole((1, C)),
            whole((1, C)),
            whole((1, mlp)),
            whole((1, C)),
            whole((C, C + 2 * mlp)),
        ],
        out_specs=(
            GRID_SPEC,
            per_image(mlp),
            per_image(mlp),
            per_image(C),
            per_image(C),
            per_image(C),
            per_image(C),
            per_image(C),
            whole((8, C)),
            whole((1, mlp)),
        ),
        scratch_shapes=[
            pltpu.VMEM((RAW, C), BF16),
            pltpu.VMEM((mlp, C), BF16),
            pltpu.VMEM((C, mlp), BF16),
            pltpu.VMEM((mlp, C), BF16),
            pltpu.VMEM((C, C), BF16),
        ],
        compiler_params=params(),
        cost_estimate=cost(images * 6e9, images * 4e6),
    )(count, win, merged, cotangent, order, back, *weights)


def run_attend_back(packed, soft, d_att):
    images = soft.shape[0]
    return pl.pallas_call(
        attend_back_kernel,
        grid=(images,),
        out_shape=(struct(packed.shape, BF16), struct((HEADS, ROWS, ROWS), F32)),
        in_specs=[
            per_image(3 * C),
            pl.BlockSpec((1, HEADS, ROWS, ROWS), lambda i: (i, 0, 0, 0)),
            per_image(C),
        ],
        out_specs=(per_image(3 * C), whole((HEADS, ROWS, ROWS))),
        compiler_params=params(),
        cost_estimate=cost(images * 6e9, images * 6e6),
    )(packed, soft, d_att)


def run_input(d_packed, win, d_res, gain, weight, back, shape):
    return pl.pallas_call(
        input_kernel,
        grid=(shape[0],),
        out_shape=(struct(shape, F32), struct((8, C), F32), struct((1, 3 * C), F32)),
        in_specs=[
            per_image(3 * C),
            per_image(C),
            per_image(C),
            whole((1, C)),
            whole((C, 3 * C)),
            whole((RAW, ROWS)),
        ],
        out_specs=(GRID_SPEC, whole((8, C)), whole((1, 3 * C))),
        scratch_shapes=[pltpu.VMEM((3 * C, C), BF16)],
        compiler_params=params(),
        cost_estimate=cost(shape[0] * 1e9, shape[0] * 2e6),
    )(d_packed, win, d_res, gain, weight, back)


def weight_grad(rows_in, rows_out):
    return lax.dot_general(
        rows_in, rows_out, (((0,), (0,)), ((), ())), preferred_element_type=F32
    ).astype(BF16)


def gather(shard):
    return lax.all_gather(shard, "fsdp", axis=0, tiled=True)


def swap(value, axis, bits):
    return lax.ppermute(value, axis, [(i, i ^ bits) for i in range(lax.axis_size(axis))])


def pick(value, index, axis):
    return lax.dynamic_index_in_dim(value, index, axis, keepdims=False)


def gather_line(shard):
    half = shard.shape[0] // 2
    own = lax.dynamic_slice_in_dim(shard, lax.axis_index("rep") % 2 * half, half, 0)
    return jnp.concatenate([own] + [swap(own, "fsdp", d) for d in (2, 4, 6)], axis=0)


def gather_pieces(line, rows):
    mine, core = lax.axis_index("fsdp"), lax.axis_index("rep") % 2
    across = swap(line, "fsdp", 1)
    pieces = [line, swap(line, "rep", 1), across, swap(across, "rep", 1)]
    starts = []
    for side in (0, 1):
        for other in (0, 1):
            for d in (0, 2, 4, 6):
                starts.append((mine ^ d ^ side) * rows + (core ^ other) * (rows // 2))
    return jnp.stack(starts).astype(jnp.int32), pieces


def gather_vector(line):
    mine, owners = lax.axis_index("fsdp"), lax.axis_size("fsdp")
    held = jnp.concatenate([line, swap(line, "fsdp", 1)], axis=0)
    stacked = held.reshape(owners, -1).astype(F32)
    order = jnp.asarray((0, 4, 2, 6, 1, 5, 3, 7))
    chosen = (jnp.arange(owners)[:, None] ^ order[None, :]) == mine
    return jnp.sum(jnp.where(chosen[:, :, None], stacked[None], 0.0), axis=1)


def gather_joined(weight_out, weight_exp, weight_red):
    replica, replicas = lax.axis_index("rep"), lax.axis_size("rep")
    rows = weight_out.shape[0] // replicas
    blocks = weight_red.shape[0] // weight_out.shape[0]

    def quarter(shard):
        size = shard.shape[0] // replicas
        return lax.dynamic_slice_in_dim(shard, replica * size, size, 0)

    red = quarter(weight_red).reshape(blocks, rows, C).transpose(1, 0, 2).reshape(rows, blocks * C)
    joined = jnp.concatenate([quarter(weight_out), quarter(weight_exp), red], axis=1)
    return lax.all_gather(joined, ("fsdp", "rep"), axis=0, tiled=True)


def halves(block, bit, axis):
    return pick(block, bit, axis), pick(block, 1 - bit, axis)


def added(a, b):
    return (a.astype(F32) + b.astype(F32)).astype(BF16)


def scatter_parts(partials):
    joined = []
    for partial in partials:
        cols = partial.shape[1]
        blocks = partial.shape[0] // (32 * 16)
        quarters = partial.reshape(32, blocks, 16, cols).transpose(0, 2, 1, 3)
        joined.append(quarters.reshape(2, 2, 2, 2, 2, 16, blocks * cols))
    return jnp.concatenate(joined, axis=-1)


def scatter_bits():
    mine, replica = lax.axis_index("fsdp"), lax.axis_index("rep")
    return mine // 4, mine // 2 % 2, mine % 2, replica // 2, replica % 2


def scatter_step(kept, got, bit, axis):
    keep, away = halves(kept, bit, axis)
    got_keep, got_away = halves(got, bit, axis)
    return added(keep, got_keep), added(away, got_away)


def join_kernel(id_ref, *refs):
    groups = refs[: len(refs) - 4]
    outs = refs[len(refs) - 4 :]
    at = 0
    for g in range(0, len(groups), 2):
        col = 0
        while col < groups[g].shape[2]:
            out = outs[at]
            at += 1
            rows, cols = out.shape
            rows = rows // 4
            for e in range(4):
                start = pl.multiple_of((id_ref[0] ^ e) * rows, rows)
                for b in range(rows // 16):
                    block = groups[g + e // 2][e % 2, :, col + b * cols : col + (b + 1) * cols]
                    out[pl.ds(start + 16 * b, 16), :] = block.astype(F32)
            col += rows // 16 * cols


def run_join(pieces, shapes):
    moved = sum(6 * a * b for a, b in shapes)
    return pl.pallas_call(
        join_kernel,
        out_shape=[struct(shape, F32) for shape in shapes],
        in_specs=[SMEM_SPEC] + [pl.BlockSpec(memory_space=pltpu.VMEM)] * len(pieces),
        out_specs=[pl.BlockSpec(memory_space=pltpu.VMEM)] * len(shapes),
        compiler_params=params(),
        cost_estimate=cost(moved, moved),
    )(lax.axis_index("rep").astype(jnp.int32)[None], *pieces)


def finish(kept_mlp, away_mlp, kept, away, vector):
    far, near, side, row, _ = scatter_bits()
    kept_mlp, away_mlp = scatter_step(kept_mlp, away_mlp, near, 0)
    kept, away = scatter_step(kept, away, side, 2)
    size = vector.shape[0]
    rows = jnp.pad(vector, (0, -size % 1024)).reshape(-1, 128)
    tie = lax.optimization_barrier

    away_mlp, away, rows = tie((away_mlp, away, rows))
    total_mlp = added(kept_mlp, swap(away_mlp, "fsdp", 2))
    kept, away = scatter_step(kept, swap(away, "fsdp", 1), far, 0)
    rows = rows + swap(rows, "rep", 1)
    total_mlp, away, rows = tie((total_mlp, away, rows))
    both_mlp = jnp.stack([total_mlp, swap(total_mlp, "rep", 1)])
    kept, away = scatter_step(kept, swap(away, "fsdp", 4), near, 0)
    rows = rows + swap(rows, "rep", 2)
    both_mlp, away, rows = tie((both_mlp, away, rows))
    rest_mlp = swap(both_mlp, "rep", 2)
    total = added(kept, swap(away, "fsdp", 2))
    rows = rows + swap(rows, "fsdp", 1)
    rest_mlp, total, rows = tie((rest_mlp, total, rows))
    both = jnp.stack([total, swap(total, "rep", 1)])
    rows = rows + swap(rows, "fsdp", 4)
    both, rows = tie((both, rows))
    rest = swap(both, "rep", 2)
    rows = rows + swap(rows, "fsdp", 2)
    return [both_mlp, rest_mlp, both, rest], rows.reshape(-1)[:size]


def reduce_weight_grad(partial):
    share = lax.psum_scatter(partial, "fsdp", scatter_dimension=0, tiled=True)
    return lax.psum(share, "rep").astype(F32)


def per_device(
    inputs,
    cotangent,
    image_counts,
    region_labels,
    position_index,
    first_gain,
    first_shift,
    attend_weight,
    attend_bias,
    bias_table,
    output_weight,
    output_bias,
    second_gain,
    second_shift,
    expand_weight,
    expand_bias,
    reduce_weight,
    reduce_bias,
):
    order_host = window_order()
    order = jnp.asarray(order_host, BF16)
    back = jnp.asarray(order_host.T, BF16)
    shards = lax.axis_size("fsdp")
    mine = lax.axis_index("fsdp")
    paired = shards == 8 and lax.axis_size("rep") == 4

    window_of = jnp.arange(WINDOWS, dtype=jnp.int32)[:, None]
    codes = jnp.pad(
        (region_labels + 4 * window_of).reshape(-1), (0, ROWS - TOK), constant_values=-1
    )
    index_rows = jnp.pad(jnp.tile(position_index.T, (1, WINDOWS)), ((0, 0), (0, ROWS - TOK)))
    table = jnp.pad(bias_table.T, ((0, 0), (0, TABLE_PAD - TABLE)))
    pair = run_bias(codes, index_rows, table)

    vectors = (
        first_gain, first_shift, attend_bias, output_bias,
        second_gain, second_shift, expand_bias, reduce_bias,
    )
    sizes = [v.shape[0] for v in vectors]
    if paired:
        joined_weights = gather_joined(output_weight, expand_weight, reduce_weight)
        line = gather_line(attend_weight)
        own = jnp.concatenate(vectors).reshape(1, -1, 128)
        vector_line = own
        for bits in (4, 2):
            vector_line = jnp.concatenate([vector_line, swap(vector_line, "fsdp", bits)], axis=0)
        line, vector_line, pair = lax.optimization_barrier((line, vector_line, pair))
        joined = gather_vector(vector_line)
        starts, pieces = gather_pieces(line, attend_weight.shape[0])
        inputs, cotangent, _ = lax.optimization_barrier((inputs, cotangent, line))
    else:
        joined = gather(jnp.concatenate(vectors)).reshape(shards, sum(sizes)).astype(F32)
    cuts = np.cumsum([0] + sizes)
    full = [
        joined[:, cuts[i] : cuts[i + 1]].reshape(1, shards * sizes[i]) for i in range(len(sizes))
    ]
    gain_one, shift_one, bias_one, bias_out, gain_two, shift_two, bias_exp, bias_red = full
    bias_packed = jnp.concatenate(
        [bias_one[:, :C], jnp.zeros((1, C), F32), bias_one[:, C:]], axis=1
    )
    if not paired:
        starts, pieces = jnp.zeros((1,), jnp.int32), [gather(attend_weight)]
        red = gather(reduce_weight).reshape(C // 16, -1, 16, C).transpose(0, 2, 1, 3).reshape(C, -1)
        joined_weights = jnp.concatenate([gather(output_weight), gather(expand_weight), red], axis=1)

    win, attend_in, packed, soft, merged, weight_one = run_attend(
        inputs, order, gain_one, shift_one, starts, pieces, bias_packed, pair
    )
    (
        block_output, hidden, d_pre, expand_in, grad_low, d_res, d_branch, d_att, sums_two, d_exp_bias,
    ) = run_mlp(
        image_counts.reshape(1), win, merged, cotangent, order, back,
        (bias_out, gain_two, shift_two, bias_exp, bias_red, joined_weights),
    )
    reduce_part = weight_grad(hidden, grad_low)
    expand_part = weight_grad(expand_in, d_pre)
    output_part = weight_grad(merged, d_branch)
    if paired:
        far, _, side, row, core = scatter_bits()
        kept_mlp, away = halves(scatter_parts([output_part, expand_part, reduce_part]), core, 4)
        kept_mlp, away = scatter_step(kept_mlp, swap(away, "rep", 1), row, 3)
        d_att, away = lax.optimization_barrier((d_att, away))
        got = swap(away, "rep", 2)
    d_packed, pairs = run_attend_back(packed, soft, d_att)
    if paired:
        kept_mlp, away_mlp = scatter_step(kept_mlp, got, side, 2)
        d_packed, pairs, away_mlp = lax.optimization_barrier((d_packed, pairs, away_mlp))
        got_mlp = swap(away_mlp, "fsdp", 1)
    attend_part = weight_grad(attend_in, d_packed)
    if paired:
        kept, away = halves(scatter_parts([attend_part]), core, 4)
        pairs, away = lax.optimization_barrier((pairs, away))
        got = swap(away, "rep", 1)
    table_part = run_table(pairs, index_rows)
    if paired:
        kept, away = scatter_step(kept, got, row, 3)
        kept_mlp, away_mlp = scatter_step(kept_mlp, got_mlp, far, 0)
        d_packed, away, away_mlp, table_part = lax.optimization_barrier(
            (d_packed, away, away_mlp, table_part)
        )
        got, got_mlp = swap(away, "rep", 2), swap(away_mlp, "fsdp", 4)
    input_grad, sums_one, d_packed_bias = run_input(
        d_packed, win, d_res, gain_one, weight_one, back, inputs.shape
    )
    small = (
        sums_one[0], sums_one[1], d_packed_bias[0, :C], d_packed_bias[0, 2 * C :],
        sums_two[2], sums_two[0], sums_two[1], d_exp_bias[0], sums_two[3], table_part.reshape(-1),
    )
    small_sizes = np.cumsum([0] + [s.shape[0] for s in small])
    if paired:
        pieces, summed = finish(kept_mlp, got_mlp, kept, got, jnp.concatenate(small))
        output_grad, expand_grad, reduce_grad, attend_grad = run_join(
            pieces,
            [w.shape for w in (output_weight, expand_weight, reduce_weight, attend_weight)],
        )
    else:
        output_grad, expand_grad, attend_grad, reduce_grad = (
            reduce_weight_grad(part)
            for part in (output_part, expand_part, attend_part, reduce_part)
        )
        summed = lax.psum(jnp.concatenate(small), ("fsdp", "rep"))
    parts = [summed[small_sizes[i] : small_sizes[i + 1]] for i in range(len(small))]
    parts = parts[:2] + [jnp.concatenate(parts[2:4])] + parts[4:]

    def own(vector):
        size = vector.shape[0] // shards
        return lax.dynamic_slice(vector, (mine * size,), (size,))

    table_grad = parts[8].reshape(HEADS, TABLE_PAD)[:, :TABLE].T
    return (
        block_output,
        input_grad,
        own(parts[0]),
        own(parts[1]),
        attend_grad,
        own(parts[2]),
        table_grad,
        output_grad,
        own(parts[3]),
        own(parts[4]),
        own(parts[5]),
        expand_grad,
        own(parts[6]),
        reduce_grad,
        own(parts[7]),
    )


def solution(mesh):
    images = P(("fsdp", "rep"), None, None, None)
    rows, vector = P("fsdp", None), P("fsdp")
    return jax.shard_map(
        per_device,
        mesh=mesh,
        in_specs=(
            images, images, P("fsdp", "rep"), P(), P(), vector, vector, rows, vector, P(),
            rows, vector, vector, vector, rows, vector, rows, vector,
        ),
        out_specs=(
            images, images, vector, vector, rows, vector, P(), rows, vector, vector, vector,
            rows, vector, rows, vector,
        ),
        check_vma=False,
    )
```

```python
import jax
import jax.numpy as jnp
import numpy as np
from jax import lax
from jax.experimental import pallas as pl
from jax.experimental.pallas import tpu as pltpu
from jax.sharding import PartitionSpec as P

C = 512
HEADS = 16
HEAD_DIM = 32
WIN = 7
SHIFT = 3
IMG = 14
WINDOWS = 4
TOKW = 49
TABLE = 169

TOK = IMG * IMG
ROWS = 208
RAW = 224
GROUP = 4
LANES = GROUP * HEAD_DIM
TABLE_PAD = 176

epsilon = 1e-05
blocked = -1e30
scale = HEAD_DIM ** (-0.5)
log2e = 1.4426950408889634
VMEM_BYTES = 56 * 1024 * 1024

F32 = jnp.float32
BF16 = jnp.bfloat16


def window_order():
    matrix = np.zeros((ROWS, RAW), np.float32)
    at = 0
    for wy in range(IMG // WIN):
        for wx in range(IMG // WIN):
            for ry in range(WIN):
                for rx in range(WIN):
                    gy = (wy * WIN + ry + SHIFT) % IMG
                    gx = (wx * WIN + rx + SHIFT) % IMG
                    matrix[at, 16 * gy + gx] = 1.0
                    at += 1
    return matrix


def dot(a, b):
    return jnp.dot(a, b, preferred_element_type=F32)


def dot_nt(a, b):
    return lax.dot_general(a, b, (((1,), (1,)), ((), ())), preferred_element_type=F32)


def turned(block):
    return block.astype(F32).T.astype(BF16)


def row_stats(values):
    centred = values - jnp.mean(values, axis=-1, keepdims=True)
    inverse = lax.rsqrt(jnp.mean(centred * centred, axis=-1, keepdims=True) + epsilon)
    return centred * inverse, inverse


def norm_pull(upstream, gain, unit, inverse):
    scaled = upstream * gain
    adjusted = (
        scaled
        - jnp.mean(scaled, axis=-1, keepdims=True)
        - unit * jnp.mean(scaled * unit, axis=-1, keepdims=True)
    )
    return adjusted * inverse


def column_sum(values):
    return jnp.sum(values, axis=0, keepdims=True)


def head_stack(block):
    lane = lax.broadcasted_iota(jnp.int32, block.shape, 1) // HEAD_DIM
    return jnp.concatenate(
        [jnp.where(lane == h, block, jnp.zeros_like(block)) for h in range(GROUP)], axis=0
    )


def head_pick(stacked):
    lane = lax.broadcasted_iota(jnp.int32, (ROWS, LANES), 1) // HEAD_DIM
    picked = stacked[:ROWS]
    for h in range(1, GROUP):
        picked = jnp.where(lane == h, stacked[h * ROWS : (h + 1) * ROWS], picked)
    return picked


def load_grid(grid_ref, rows_ref, order):
    @pl.when(pl.program_id(0) == 0)
    def _():
        rows_ref[...] = jnp.zeros_like(rows_ref)

    images = grid_ref.shape[0]
    for i in range(images):
        for r in range(IMG):
            at = RAW * i + 16 * r
            rows_ref[at : at + IMG, :] = grid_ref[i, r]
    return jnp.concatenate(
        [dot(order, rows_ref[RAW * i : RAW * (i + 1), :]) for i in range(images)], axis=0
    )


def chunk_place(j):
    return j % 2 * 8 + j // 2 % 2 * 4 + j // 8 * 2 + j // 4 % 2


def write_chunks(outs, core, sums_ref, col):
    cols = sums_ref.shape[1]
    for j in range(sums_ref.shape[0] // 32):
        for out, bit in zip(outs, (core, 1 - core)):
            start = pl.multiple_of(16 * (2 * j + bit), 16)
            out[chunk_place(j), :, col : col + cols] = sums_ref[pl.ds(start, 16), :].astype(BF16)


def bias_kernel(code_ref, codes_ref, index_ref, table_ref, out_ref):
    out_ref[...] = jnp.full(out_ref.shape, blocked, F32)
    entry = lax.broadcasted_iota(jnp.int32, (TABLE_PAD, ROWS), 0)
    codes = codes_ref[...]
    table = table_ref[...]
    for j in range(TOKW):
        hot = (entry == index_ref[j : j + 1, :]).astype(F32).astype(BF16)
        found = dot(table, hot) * log2e
        for w in range(WINDOWS):
            row = TOKW * w + j
            out_ref[:, row, :] = jnp.where(codes == code_ref[row], found, blocked)


def table_kernel(sums_ref, index_ref, out_ref, window_ref):
    for h in range(HEADS):
        part = sums_ref[h, :TOKW, :]
        for w in range(1, WINDOWS):
            part = part + sums_ref[h, TOKW * w : TOKW * (w + 1), :]
        window_ref[h, :TOKW, :] = part
    entry = lax.broadcasted_iota(jnp.int32, (TABLE_PAD, ROWS), 0)
    total = jnp.zeros((2 * HEADS, TABLE_PAD), F32)
    for j in range(TOKW):
        part = window_ref[:, j, :]
        hot = (entry == index_ref[j : j + 1, :]).astype(F32).astype(BF16)
        high = part.astype(BF16)
        low = (part - high.astype(F32)).astype(BF16)
        total = total + dot_nt(jnp.concatenate([high, low], axis=0), hot)
    out_ref[...] = total[:HEADS] + total[HEADS:]


def attend_kernel(starts_ref, grid_ref, order_ref, rows_in_ref, bias_ref, pair_ref, *rest):
    pieces = rest[:-7]
    win_ref, in_ref, packed_ref, soft_ref, merged_ref, weight_ref, rows_ref = rest[-7:]

    @pl.when(pl.program_id(0) == 0)
    def _():
        rows = weight_ref.shape[0] // starts_ref.shape[0]
        at = 0
        for piece in pieces:
            for r in range(0, piece.shape[0], rows):
                start = pl.multiple_of(starts_ref[at], rows)
                weight_ref[pl.ds(start, rows), :] = piece[r : r + rows, :]
                at += 1

    values = load_grid(grid_ref, rows_ref, order_ref[...])
    win_ref[...] = values.astype(BF16)
    unit, _ = row_stats(values)
    attend_in = (unit * rows_in_ref[0:1, :] + rows_in_ref[1:2, :]).astype(BF16)
    in_ref[...] = attend_in
    packed_ref[...] = (dot(attend_in, weight_ref[...]) + bias_ref[...]).astype(BF16)
    for g in range(HEADS // GROUP):
        at = LANES * g
        q = packed_ref[:, at : at + LANES]
        k = packed_ref[:, C + at : C + at + LANES]
        v_turned = turned(packed_ref[:, 2 * C + at : 2 * C + at + LANES])
        raw = dot_nt(head_stack(k), q)
        parts = []
        for h in range(GROUP):
            s = raw[h * ROWS : (h + 1) * ROWS] * (scale * log2e) + pair_ref[g * GROUP + h]
            e = jnp.exp2(s - jnp.max(s, axis=0, keepdims=True))
            p = (e * (1.0 / column_sum(e))).astype(BF16)
            soft_ref[0, g * GROUP + h] = p
            parts.append(dot(v_turned[h * HEAD_DIM : (h + 1) * HEAD_DIM], p))
        merged_ref[:, at : at + LANES] = jnp.concatenate(parts, axis=0).T.astype(BF16)


def mlp_kernel(
    count_ref, win_ref, merged_ref, grid_ref, order_ref, back_ref, six_ref, exp_b_ref, joined_ref,
    block_ref, d_res_ref, d_att_ref, kept_ref, away_ref,
    sums_ref, wide_ref, rows_ref, red_w_ref, out_sum_ref, exp_sum_ref, red_sum_ref,
):
    step_at = pl.program_id(0)
    images = grid_ref.shape[0]
    out_b, gain, shift, red_b = (six_ref[r : r + 1, :] for r in (2, 3, 4, 5))
    mlp = exp_b_ref.shape[1]
    blocks = mlp // C
    out_w_ref = joined_ref.at[:, :C]
    exp_w_ref = joined_ref.at[:, C : C + mlp]

    @pl.when(step_at == 0)
    def _():
        out_sum_ref[...] = jnp.zeros_like(out_sum_ref)
        exp_sum_ref[...] = jnp.zeros_like(exp_sum_ref)
        red_sum_ref[...] = jnp.zeros_like(red_sum_ref)
        sums_ref[...] = jnp.zeros_like(sums_ref)
        wide_ref[...] = jnp.zeros_like(wide_ref)
        for at in range(0, C, 16):
            for b in range(blocks):
                cols = C + mlp + b * C
                red_w_ref[blocks * at + 16 * b : blocks * at + 16 * (b + 1), :] = joined_ref[
                    at : at + 16, cols : cols + C
                ]

    row = lax.broadcasted_iota(jnp.int32, (images * ROWS, 1), 0)
    live = (row < (count_ref[0] - images * step_at) * ROWS).astype(F32)
    grad = load_grid(grid_ref, rows_ref, order_ref[...]) * live
    grad_low = grad.astype(BF16)
    grad_turned = turned(grad_low)
    residual = win_ref[...].astype(F32) + dot(merged_ref[...], out_w_ref[...]) + out_b
    unit, inverse = row_stats(residual)
    expand_in = (unit * gain + shift).astype(BF16)
    in_turned = turned(expand_in)
    step = 512
    out = residual + red_b
    d_in = jnp.zeros((images * ROWS, C), F32)
    for m in range(0, mlp, step):
        cols = slice(m, m + step)
        pre = dot(expand_in, exp_w_ref[:, cols]) + exp_b_ref[:, cols]
        bell = jnp.exp(pre * pre * -0.5)
        t = 1.0 / (1.0 + jnp.abs(pre) * (0.3275911 * 0.7071067811865476))
        tail = (
            t
            * bell
            * (
                0.127414796
                + t * (-0.142248368 + t * (0.7107068705 + t * (-0.7265760135 + t * 0.5307027145)))
            )
        )
        cdf = jnp.where(pre >= 0, 1.0 - tail, tail)
        hidden = (pre * cdf).astype(BF16)
        red_sum_ref[:, cols] += dot(grad_turned, hidden)
        d_hidden = dot_nt(grad_low, red_w_ref[cols, :])
        d_pre = (d_hidden * (cdf + pre * bell * 0.3989422804014327)).astype(BF16)
        exp_sum_ref[:, cols] += dot(in_turned, d_pre)
        wide_ref[:, cols] += column_sum(d_pre.astype(F32))
        out = out + dot(hidden, red_w_ref[cols, :])
        d_in = d_in + dot_nt(d_pre, exp_w_ref[:, cols])
    block = (out * live).astype(BF16)
    for i in range(images):
        block_rows = dot(back_ref[...], block[ROWS * i : ROWS * (i + 1)]).astype(BF16)
        for r in range(IMG):
            block_ref[i, r] = block_rows[16 * r : 16 * r + IMG]
    d_res = grad + norm_pull(d_in, gain, unit, inverse)
    d_res_ref[...] = d_res
    d_branch = d_res.astype(BF16)
    d_att_ref[...] = dot_nt(d_branch, out_w_ref[...]).astype(BF16)
    out_sum_ref[...] += dot(turned(merged_ref[...]), d_branch)
    sums_ref[0:1, :] += column_sum(d_in * unit)
    sums_ref[1:2, :] += column_sum(d_in)
    sums_ref[2:3, :] += column_sum(d_branch.astype(F32))
    sums_ref[3:4, :] += column_sum(grad)

    @pl.when(step_at == pl.num_programs(0) - 1)
    def _():
        core = count_ref[1]
        outs = (kept_ref, away_ref)
        write_chunks(outs, core, out_sum_ref, 0)
        write_chunks(outs, core, exp_sum_ref, C)
        for m in range(0, mlp, C):
            red_w_ref[m : m + C, :] = red_sum_ref[:, m : m + C].T.astype(BF16)
        for j in range(C // 32):
            for out, bit in zip(outs, (core, 1 - core)):
                for b in range(blocks):
                    start = pl.multiple_of(16 * (blocks * (2 * j + bit) + b), 16)
                    at = C + mlp + b * C
                    out[chunk_place(j), :, at : at + C] = red_w_ref[pl.ds(start, 16), :]


def attend_back_kernel(
    core_ref, packed_ref, soft_ref, d_att_ref, in_ref,
    d_packed_ref, pairs_ref, kept_ref, away_ref, sum_ref,
):
    @pl.when(pl.program_id(0) == 0)
    def _():
        pairs_ref[...] = jnp.zeros_like(pairs_ref)
        sum_ref[...] = jnp.zeros_like(sum_ref)

    for g in range(HEADS // GROUP):
        at = LANES * g
        q = packed_ref[:, at : at + LANES]
        k_turned = turned(packed_ref[:, C + at : C + at + LANES])
        v = packed_ref[:, 2 * C + at : 2 * C + at + LANES]
        d_att = d_att_ref[:, at : at + LANES]
        d_soft = dot_nt(head_stack(v), d_att)
        d_raw, d_q, soft = [], [], []
        for h in range(GROUP):
            head = g * GROUP + h
            low = soft_ref[0, head]
            soft.append(low)
            p = low.astype(F32)
            dp = d_soft[h * ROWS : (h + 1) * ROWS]
            ds = (p * (dp - column_sum(p * dp))).astype(BF16)
            pairs_ref[head] += ds.astype(F32)
            d_raw.append(ds)
            d_q.append(dot(k_turned[h * HEAD_DIM : (h + 1) * HEAD_DIM], ds))
        d_k = head_pick(dot(jnp.concatenate(d_raw, axis=0), q))
        d_v = head_pick(dot(jnp.concatenate(soft, axis=0), d_att))
        d_packed_ref[:, at : at + LANES] = (jnp.concatenate(d_q, axis=0) * scale).T.astype(BF16)
        d_packed_ref[:, C + at : C + at + LANES] = (d_k * scale).astype(BF16)
        d_packed_ref[:, 2 * C + at : 2 * C + at + LANES] = d_v.astype(BF16)
    in_turned = turned(in_ref[...])
    for m in range(0, 3 * C, C):
        sum_ref[:, m : m + C] += dot(in_turned, d_packed_ref[:, m : m + C])

    @pl.when(pl.program_id(0) == pl.num_programs(0) - 1)
    def _():
        write_chunks((kept_ref, away_ref), core_ref[0], sum_ref, 0)


def input_kernel(
    d_packed_ref, win_ref, d_res_ref, six_ref, weight_ref, back_ref,
    grad_ref, sums_ref, wide_ref, turned_ref,
):
    @pl.when(pl.program_id(0) == 0)
    def _():
        for m in range(0, 3 * C, C):
            turned_ref[m : m + C, :] = turned(weight_ref[:, m : m + C])
        sums_ref[...] = jnp.zeros_like(sums_ref)
        wide_ref[...] = jnp.zeros_like(wide_ref)

    d_packed = d_packed_ref[...]
    d_in = dot(d_packed, turned_ref[...])
    unit, inverse = row_stats(win_ref[...].astype(F32))
    total = d_res_ref[...] + norm_pull(d_in, six_ref[0:1, :], unit, inverse)
    sums_ref[0:1, :] += column_sum(d_in * unit)
    sums_ref[1:2, :] += column_sum(d_in)
    wide_ref[...] += column_sum(d_packed.astype(F32))
    high = total.astype(BF16)
    low = (total - high.astype(F32)).astype(BF16)
    rows = dot(back_ref[...], high) + dot(back_ref[...], low)
    for r in range(IMG):
        grad_ref[0, r] = rows[16 * r : 16 * r + IMG]


def whole(shape):
    return pl.BlockSpec(shape, lambda *_: (0,) * len(shape))


def per_image(width):
    return pl.BlockSpec((ROWS, width), lambda i: (i, 0))


GRID_SPEC = pl.BlockSpec((1, IMG, IMG, C), lambda i: (i, 0, 0, 0))
SMEM_SPEC = pl.BlockSpec(memory_space=pltpu.SMEM)


def params():
    return pltpu.CompilerParams(vmem_limit_bytes=VMEM_BYTES)


def cost(flops, moved, special=0):
    return pl.CostEstimate(flops=int(flops), bytes_accessed=int(moved), transcendentals=int(special))


def struct(shape, dtype):
    return jax.ShapeDtypeStruct(shape, dtype)


def run_bias(codes, index_rows, table):
    return pl.pallas_call(
        bias_kernel,
        out_shape=struct((HEADS, ROWS, ROWS), F32),
        in_specs=[SMEM_SPEC] + [pl.BlockSpec(memory_space=pltpu.VMEM)] * 3,
        out_specs=pl.BlockSpec(memory_space=pltpu.VMEM),
        compiler_params=params(),
        cost_estimate=cost(2e9, 4e6),
    )(codes, codes[None, :], index_rows, table)


def run_table(pairs, index_rows):
    return pl.pallas_call(
        table_kernel,
        out_shape=struct((HEADS, TABLE_PAD), F32),
        in_specs=[pl.BlockSpec(memory_space=pltpu.VMEM)] * 2,
        out_specs=pl.BlockSpec(memory_space=pltpu.VMEM),
        scratch_shapes=[pltpu.VMEM((HEADS, 56, ROWS), F32)],
        compiler_params=params(),
        cost_estimate=cost(2e9, 4e6),
    )(pairs, index_rows)


def run_attend(inputs, order, six, starts, pieces, bias, pair):
    images = inputs.shape[0]
    rows = images * ROWS
    return pl.pallas_call(
        attend_kernel,
        grid=(images,),
        out_shape=(
            struct((rows, C), BF16),
            struct((rows, C), BF16),
            struct((rows, 3 * C), BF16),
            struct((images, HEADS, ROWS, ROWS), BF16),
            struct((rows, C), BF16),
            struct((C, 3 * C), BF16),
        ),
        in_specs=[
            SMEM_SPEC,
            GRID_SPEC,
            whole((ROWS, RAW)),
            whole((6, C)),
            whole((1, 3 * C)),
            whole((HEADS, ROWS, ROWS)),
        ]
        + [whole(piece.shape) for piece in pieces],
        out_specs=(
            per_image(C),
            per_image(C),
            per_image(3 * C),
            pl.BlockSpec((1, HEADS, ROWS, ROWS), lambda i: (i, 0, 0, 0)),
            per_image(C),
            whole((C, 3 * C)),
        ),
        scratch_shapes=[pltpu.VMEM((RAW, C), BF16)],
        compiler_params=params(),
        cost_estimate=cost(images * 5e9, images * 6e6),
    )(starts, inputs, order, six, bias, pair, *pieces)


def run_mlp(count, win, merged, cotangent, order, back, weights):
    images = cotangent.shape[0]
    rows = images * ROWS
    mlp = weights[1].shape[1]
    per = 2 if images % 2 == 0 else 1
    some = pl.BlockSpec((per * ROWS, C), lambda i: (i, 0))
    grids = pl.BlockSpec((per, IMG, IMG, C), lambda i: (i, 0, 0, 0))
    half = (C // 32, 16, C + 2 * mlp)
    return pl.pallas_call(
        mlp_kernel,
        grid=(images // per,),
        out_shape=(
            struct(cotangent.shape, BF16),
            struct((rows, C), F32),
            struct((rows, C), BF16),
            struct(half, BF16),
            struct(half, BF16),
            struct((8, C), F32),
            struct((1, mlp), F32),
        ),
        in_specs=[
            SMEM_SPEC,
            some,
            some,
            grids,
            whole((ROWS, RAW)),
            whole((RAW, ROWS)),
            whole((6, C)),
            whole((1, mlp)),
            whole((C, C + 2 * mlp)),
        ],
        out_specs=(grids, some, some, whole(half), whole(half), whole((8, C)), whole((1, mlp))),
        scratch_shapes=[
            pltpu.VMEM((per * RAW, C), BF16),
            pltpu.VMEM((mlp, C), BF16),
            pltpu.VMEM((C, C), F32),
            pltpu.VMEM((C, mlp), F32),
            pltpu.VMEM((C, mlp), F32),
        ],
        compiler_params=params(),
        cost_estimate=cost(images * 6e9, images * 4e6),
    )(count, win, merged, cotangent, order, back, *weights)


def run_attend_back(core, packed, soft, d_att, attend_in):
    images = soft.shape[0]
    half = (C // 32, 16, 3 * C)
    return pl.pallas_call(
        attend_back_kernel,
        grid=(images,),
        out_shape=(
            struct(packed.shape, BF16),
            struct((HEADS, ROWS, ROWS), F32),
            struct(half, BF16),
            struct(half, BF16),
        ),
        in_specs=[
            SMEM_SPEC,
            per_image(3 * C),
            pl.BlockSpec((1, HEADS, ROWS, ROWS), lambda i: (i, 0, 0, 0)),
            per_image(C),
            per_image(C),
        ],
        out_specs=(per_image(3 * C), whole((HEADS, ROWS, ROWS)), whole(half), whole(half)),
        scratch_shapes=[pltpu.VMEM((C, 3 * C), F32)],
        compiler_params=params(),
        cost_estimate=cost(images * 6e9, images * 6e6),
    )(core, packed, soft, d_att, attend_in)


def run_input(d_packed, win, d_res, six, weight, back, shape):
    return pl.pallas_call(
        input_kernel,
        grid=(shape[0],),
        out_shape=(struct(shape, F32), struct((8, C), F32), struct((1, 3 * C), F32)),
        in_specs=[
            per_image(3 * C),
            per_image(C),
            per_image(C),
            whole((6, C)),
            whole((C, 3 * C)),
            whole((RAW, ROWS)),
        ],
        out_specs=(GRID_SPEC, whole((8, C)), whole((1, 3 * C))),
        scratch_shapes=[pltpu.VMEM((3 * C, C), BF16)],
        compiler_params=params(),
        cost_estimate=cost(shape[0] * 1e9, shape[0] * 2e6),
    )(d_packed, win, d_res, six, weight, back)


def gather(shard):
    return lax.all_gather(shard, "fsdp", axis=0, tiled=True)


def swap(value, axis, bits):
    return lax.ppermute(value, axis, [(i, i ^ bits) for i in range(lax.axis_size(axis))])


def pick(value, index, axis):
    return lax.dynamic_index_in_dim(value, index, axis, keepdims=False)


def gather_line(shard):
    half = shard.shape[0] // 2
    own = lax.dynamic_slice_in_dim(shard, lax.axis_index("rep") % 2 * half, half, 0)
    return jnp.concatenate([own] + [swap(own, "fsdp", d) for d in (2, 4, 6)], axis=0)


def gather_pieces(line, rows, vector_line):
    mine, core = lax.axis_index("fsdp"), lax.axis_index("rep") % 2
    across = swap(line, "fsdp", 1)
    vector = jnp.concatenate([vector_line, swap(vector_line, "fsdp", 1)], axis=0)
    across, vector = lax.optimization_barrier((across, vector))
    pieces = [line, swap(line, "rep", 1), across, swap(across, "rep", 1)]
    starts = []
    for side in (0, 1):
        for other in (0, 1):
            for d in (0, 2, 4, 6):
                starts.append((mine ^ d ^ side) * rows + (core ^ other) * (rows // 2))
    return jnp.stack(starts).astype(jnp.int32), pieces, gather_vector(vector)


def gather_vector(held):
    mine, owners = lax.axis_index("fsdp"), lax.axis_size("fsdp")
    stacked = held.reshape(owners, -1).astype(F32)
    order = jnp.asarray((0, 4, 2, 6, 1, 5, 3, 7))
    chosen = (jnp.arange(owners)[:, None] ^ order[None, :]) == mine
    return jnp.sum(jnp.where(chosen[:, :, None], stacked[None], 0.0), axis=1)


def gather_joined(weight_out, weight_exp, weight_red):
    replica, replicas = lax.axis_index("rep"), lax.axis_size("rep")
    rows = weight_out.shape[0] // replicas
    blocks = weight_red.shape[0] // weight_out.shape[0]

    def quarter(shard):
        size = shard.shape[0] // replicas
        return lax.dynamic_slice_in_dim(shard, replica * size, size, 0)

    red = quarter(weight_red).reshape(blocks, rows, C).transpose(1, 0, 2).reshape(rows, blocks * C)
    joined = jnp.concatenate([quarter(weight_out), quarter(weight_exp), red], axis=1)
    return lax.all_gather(joined, ("fsdp", "rep"), axis=0, tiled=True)


def halves(block, bit, axis):
    return pick(block, bit, axis), pick(block, 1 - bit, axis)


def added(a, b):
    return (a.astype(F32) + b.astype(F32)).astype(BF16)


def chunk_rows(kept, away):
    chunks = jnp.stack([kept, away]).reshape(2, 2, 2, 2, 2, 16, -1)
    return chunks.transpose(3, 4, 2, 1, 0, 5, 6).reshape(C, -1)


def scatter_bits():
    mine, replica = lax.axis_index("fsdp"), lax.axis_index("rep")
    return mine // 4, mine // 2 % 2, mine % 2, replica // 2, replica % 2


def scatter_step(kept, got, bit):
    keep, away = halves(kept, bit, 0)
    got_keep, got_away = halves(got, bit, 0)
    return added(keep, got_keep), added(away, got_away)


def join_kernel(ids_ref, both_ref, rest_ref, *refs):
    parts, rows_ref = refs[:4], refs[4]
    outs, vectors = refs[5:9], refs[9:]
    at = 0
    for out in outs:
        rows, cols = out.shape
        rows = rows // 4
        for e in range(4):
            start = pl.multiple_of((ids_ref[0] ^ e) * rows, rows)
            for b in range(rows // 16):
                if out is outs[3]:
                    block = parts[e][...]
                else:
                    block = (both_ref, rest_ref)[e // 2][e % 2, :, at + b * cols : at + (b + 1) * cols]
                out[pl.ds(start + 16 * b, 16), :] = block.astype(F32)
        at += rows // 16 * cols
    mine = ids_ref[1]
    base = 0
    for vector in vectors:
        if vector.shape[1] < 128:
            row = rows_ref[pl.ds(base + mine // 2, 1), :]
            moved = jnp.concatenate([row[:, 64:], row[:, :64]], axis=1)
            vector[...] = jnp.where(mine % 2 == 1, moved, row)[:, :64]
            base += 4
        else:
            count = vector.shape[0]
            for r in range(count):
                vector[r : r + 1, :] = rows_ref[pl.ds(base + count * mine + r, 1), :]
            base += 8 * count


def run_join(mlp, parts, rows, shapes, sizes):
    ids = jnp.stack([lax.axis_index("rep"), lax.axis_index("fsdp")]).astype(jnp.int32)
    moved = sum(6 * a * b for a, b in shapes)
    flat = [(max(size // 128, 1), min(size, 128)) for size in sizes]
    count = len(shapes) + len(sizes)
    outs = pl.pallas_call(
        join_kernel,
        out_shape=[struct(shape, F32) for shape in list(shapes) + flat],
        in_specs=[SMEM_SPEC] + [pl.BlockSpec(memory_space=pltpu.VMEM)] * 7,
        out_specs=[pl.BlockSpec(memory_space=pltpu.VMEM)] * count,
        compiler_params=params(),
        cost_estimate=cost(moved, moved),
    )(ids, *mlp, *parts, rows)
    return outs[:4], [out.reshape(-1) for out in outs[4:]]


def finish(kept_mlp, got_mlp, kept, got, vector, results):
    far, near, side, _, _ = scatter_bits()
    line = lax.axis_index("fsdp") // 2
    tie = lax.optimization_barrier
    kept_mlp, got_mlp, kept, got, vector = tie((kept_mlp, got_mlp, kept, got, vector))
    kept_mlp, away_mlp = scatter_step(kept_mlp, got_mlp, far)
    kept, away = scatter_step(kept, got, side)
    rows = jnp.pad(jnp.concatenate(vector), (0, -sum(v.shape[0] for v in vector) % 1024))
    rows = rows.reshape(-1, 128)

    away_mlp, away, rows = tie((away_mlp, away, rows))
    got_mlp = swap(away_mlp, "fsdp", 4)
    total = added(kept, swap(away, "fsdp", 1)).reshape(4, kept.shape[-2], kept.shape[-1])
    own = pick(total, line, 0)
    pieces = [pick(total, line ^ d, 0) for d in (1, 2, 3)]
    rows = rows + swap(rows, "rep", 1)

    own, pieces, rows, results = tie((own, pieces, rows, results))
    results = tuple(result.transpose(1, 2, 0, 3) for result in results)
    got_pieces = [swap(pieces[d - 1], "fsdp", 2 * d) for d in (1, 2, 3)]
    rows = rows + swap(rows, "rep", 2)

    got_mlp, kept_mlp, rows, results = tie((got_mlp, kept_mlp, rows, results))
    kept_mlp, away_mlp = scatter_step(kept_mlp, got_mlp, near)
    total_mlp = added(kept_mlp, swap(away_mlp, "fsdp", 2))
    rows = rows + swap(rows, "fsdp", 1)
    total = own.astype(F32)
    for piece in got_pieces:
        total = total + piece.astype(F32)
    total = total.astype(BF16)

    total, total_mlp, rows = tie((total, total_mlp, rows))
    parts = [total] + [swap(total, "rep", e) for e in (1, 2, 3)]
    both_mlp = jnp.stack([total_mlp, swap(total_mlp, "rep", 1)])
    rows = rows + swap(rows, "fsdp", 4)

    both_mlp, parts, rows = tie((both_mlp, parts, rows))
    rest_mlp = swap(both_mlp, "rep", 2)
    rows = rows + swap(rows, "fsdp", 2)
    results = tuple(result.transpose(2, 0, 1, 3) for result in results)
    return [both_mlp, rest_mlp], parts, rows, results


def reduce_weight_grad(partial):
    share = lax.psum_scatter(partial, "fsdp", scatter_dimension=0, tiled=True)
    return lax.psum(share, "rep").astype(F32)


def per_device(
    inputs,
    cotangent,
    image_counts,
    region_labels,
    position_index,
    first_gain,
    first_shift,
    attend_weight,
    attend_bias,
    bias_table,
    output_weight,
    output_bias,
    second_gain,
    second_shift,
    expand_weight,
    expand_bias,
    reduce_weight,
    reduce_bias,
):
    order_host = window_order()
    order = jnp.asarray(order_host, BF16)
    back = jnp.asarray(order_host.T, BF16)
    shards = lax.axis_size("fsdp")
    mine = lax.axis_index("fsdp")
    paired = shards == 8 and lax.axis_size("rep") == 4

    window_of = jnp.arange(WINDOWS, dtype=jnp.int32)[:, None]
    codes = jnp.pad(
        (region_labels + 4 * window_of).reshape(-1), (0, ROWS - TOK), constant_values=-1
    )
    index_rows = jnp.pad(jnp.tile(position_index.T, (1, WINDOWS)), ((0, 0), (0, ROWS - TOK)))
    table = jnp.pad(bias_table.T, ((0, 0), (0, TABLE_PAD - TABLE)))
    vectors = (
        first_gain, first_shift, output_bias, second_gain, second_shift, reduce_bias,
        attend_bias, expand_bias,
    )
    sizes = [v.shape[0] for v in vectors]
    if paired:
        joined_weights = gather_joined(output_weight, expand_weight, reduce_weight)
        line = gather_line(attend_weight)
        own = jnp.concatenate(vectors).reshape(1, -1, 128)
        vector_line = jnp.concatenate([own, swap(own, "fsdp", 4)], axis=0)
        line, vector_line, codes = lax.optimization_barrier((line, vector_line, codes))
        vector_line = jnp.concatenate([vector_line, swap(vector_line, "fsdp", 2)], axis=0)
        starts, pieces, joined = gather_pieces(line, attend_weight.shape[0], vector_line)
        inputs, cotangent, _ = lax.optimization_barrier((inputs, cotangent, line))
    else:
        joined = gather(jnp.concatenate(vectors)).reshape(shards, sum(sizes)).astype(F32)
    pair = run_bias(codes, index_rows, table)
    pair = run_bias(codes, index_rows, table)
    six = joined[:, : 6 * sizes[0]].reshape(shards, 6, sizes[0]).transpose(1, 0, 2).reshape(6, C)
    bias_one = joined[:, 6 * sizes[0] : 6 * sizes[0] + sizes[6]].reshape(1, 2 * C)
    bias_exp = joined[:, 6 * sizes[0] + sizes[6] :].reshape(1, shards * sizes[7])
    bias_packed = jnp.concatenate(
        [bias_one[:, :C], jnp.zeros((1, C), F32), bias_one[:, C:]], axis=1
    )
    if not paired:
        starts, pieces = jnp.zeros((1,), jnp.int32), [gather(attend_weight)]
        red = gather(reduce_weight).reshape(C // 16, -1, 16, C).transpose(0, 2, 1, 3).reshape(C, -1)
        joined_weights = jnp.concatenate([gather(output_weight), gather(expand_weight), red], axis=1)

    win, attend_in, packed, soft, merged, weight_one = run_attend(
        inputs, order, six, starts, pieces, bias_packed, pair
    )
    far, _, side, row, core = scatter_bits()
    core = core if paired else jnp.zeros((), jnp.int32)
    block_output, d_res, d_att, kept_mlp, away_mlp, sums_two, d_exp_bias = run_mlp(
        jnp.stack([image_counts[0, 0], core]), win, merged, cotangent, order, back,
        (six, bias_exp, joined_weights),
    )
    if paired:
        split = (2, 2, 2, 2, 16, -1)
        kept_mlp, away = kept_mlp.reshape(split), away_mlp.reshape(split)
        kept_mlp, away = scatter_step(kept_mlp, swap(away, "rep", 1), row)
        d_att, away = lax.optimization_barrier((d_att, away))
        got = swap(away, "rep", 2)
    d_packed, pairs, kept, away = run_attend_back(core[None], packed, soft, d_att, attend_in)
    if paired:
        kept_mlp, away_mlp = scatter_step(kept_mlp, got, side)
        pairs, away, away_mlp = lax.optimization_barrier((pairs, away, away_mlp))
        kept, away = kept.reshape(split), away.reshape(split)
        got, got_mlp = swap(away, "rep", 1), swap(away_mlp, "fsdp", 1)
    table_part = run_table(pairs, index_rows)
    if paired:
        kept, away = scatter_step(kept, got, row)
        d_packed, away, table_part = lax.optimization_barrier((d_packed, away, table_part))
        got = swap(away, "rep", 2)
    input_grad, sums_one, d_packed_bias = run_input(
        d_packed, win, d_res, six, weight_one, back, inputs.shape
    )
    small = (
        sums_one[0], sums_one[1], sums_two[2], sums_two[0], sums_two[1], sums_two[3],
        d_packed_bias[0, :C], d_packed_bias[0, 2 * C :], d_exp_bias[0], table_part.reshape(-1),
    )
    if paired:
        mlp_pieces, part_pieces, rows, (block_output, input_grad) = finish(
            kept_mlp, got_mlp, kept, got, small, (block_output, input_grad)
        )
        (output_grad, expand_grad, reduce_grad, attend_grad), owned = run_join(
            mlp_pieces, part_pieces, rows,
            [w.shape for w in (output_weight, expand_weight, reduce_weight, attend_weight)],
            sizes,
        )
        table_sum = rows.reshape(-1)[sum(sizes) * shards :][: HEADS * TABLE_PAD]
    else:
        parts = chunk_rows(kept_mlp, away_mlp)
        mlp = bias_exp.shape[1]
        reduce_part = parts[:, C + mlp :].reshape(C // 16, 16, -1, C).transpose(0, 2, 1, 3)
        output_grad, expand_grad, attend_grad, reduce_grad = (
            reduce_weight_grad(part)
            for part in (
                parts[:, :C], parts[:, C : C + mlp], chunk_rows(kept, away), reduce_part.reshape(mlp, C),
            )
        )
        summed = lax.psum(jnp.concatenate(small), ("fsdp", "rep"))
        ends = np.cumsum([0] + [size * shards for size in sizes])
        owned = [
            lax.dynamic_slice(summed[ends[i] : ends[i + 1]], (mine * sizes[i],), (sizes[i],))
            for i in range(len(sizes))
        ]
        table_sum = summed[ends[-1] :]
    table_grad = table_sum.reshape(HEADS, TABLE_PAD)[:, :TABLE].T
    return (
        block_output,
        input_grad,
        owned[0],
        owned[1],
        attend_grad,
        owned[6],
        table_grad,
        output_grad,
        owned[2],
        owned[3],
        owned[4],
        expand_grad,
        owned[7],
        reduce_grad,
        owned[5],
    )


def solution(mesh):
    images = P(("fsdp", "rep"), None, None, None)
    rows, vector = P("fsdp", None), P("fsdp")
    return jax.shard_map(
        per_device,
        mesh=mesh,
        in_specs=(
            images, images, P("fsdp", "rep"), P(), P(), vector, vector, rows, vector, P(),
            rows, vector, vector, vector, rows, vector, rows, vector,
        ),
        out_specs=(
            images, images, vector, vector, rows, vector, P(), rows, vector, vector, vector,
            rows, vector, rows, vector,
        ),
        check_vma=False,
    )
```

```python
import jax
import jax.numpy as jnp
import numpy as np
from jax import lax
from jax.experimental import pallas as pl
from jax.experimental.layout import Layout, with_layout_constraint
from jax.experimental.pallas import tpu as pltpu
from jax.sharding import PartitionSpec as P

C = 512
HEADS = 16
HEAD_DIM = 32
WIN = 7
SHIFT = 3
IMG = 14
WINDOWS = 4
TOKW = 49
TABLE = 169

TOK = IMG * IMG
ROWS = 208
RAW = 224
GROUP = 4
LANES = GROUP * HEAD_DIM
TABLE_PAD = 176

epsilon = 1e-05
blocked = -1e30
scale = HEAD_DIM ** (-0.5)
log2e = 1.4426950408889634
VMEM_BYTES = 56 * 1024 * 1024

F32 = jnp.float32
BF16 = jnp.bfloat16


def window_order():
    matrix = np.zeros((ROWS, RAW), np.float32)
    at = 0
    for wy in range(IMG // WIN):
        for wx in range(IMG // WIN):
            for ry in range(WIN):
                for rx in range(WIN):
                    gy = (wy * WIN + ry + SHIFT) % IMG
                    gx = (wx * WIN + rx + SHIFT) % IMG
                    matrix[at, 16 * gy + gx] = 1.0
                    at += 1
    return matrix


def dot(a, b):
    return jnp.dot(a, b, preferred_element_type=F32)


def dot_nt(a, b):
    return lax.dot_general(a, b, (((1,), (1,)), ((), ())), preferred_element_type=F32)


def turned(block):
    return block.astype(F32).T.astype(BF16)


def row_stats(values):
    centred = values - jnp.mean(values, axis=-1, keepdims=True)
    inverse = lax.rsqrt(jnp.mean(centred * centred, axis=-1, keepdims=True) + epsilon)
    return centred * inverse, inverse


def norm_pull(upstream, gain, unit, inverse):
    scaled = upstream * gain
    adjusted = (
        scaled
        - jnp.mean(scaled, axis=-1, keepdims=True)
        - unit * jnp.mean(scaled * unit, axis=-1, keepdims=True)
    )
    return adjusted * inverse


def column_sum(values):
    return jnp.sum(values, axis=0, keepdims=True)


def head_stack(block):
    lane = lax.broadcasted_iota(jnp.int32, block.shape, 1) // HEAD_DIM
    return jnp.concatenate(
        [jnp.where(lane == h, block, jnp.zeros_like(block)) for h in range(GROUP)], axis=0
    )


def head_pick(stacked):
    lane = lax.broadcasted_iota(jnp.int32, (ROWS, LANES), 1) // HEAD_DIM
    picked = stacked[:ROWS]
    for h in range(1, GROUP):
        picked = jnp.where(lane == h, stacked[h * ROWS : (h + 1) * ROWS], picked)
    return picked


def load_grid(grid_ref, rows_ref, order):
    @pl.when(pl.program_id(0) == 0)
    def _():
        rows_ref[...] = jnp.zeros_like(rows_ref)

    images = grid_ref.shape[0]
    for i in range(images):
        for r in range(IMG):
            at = RAW * i + 16 * r
            rows_ref[at : at + IMG, :] = grid_ref[i, r]
    return jnp.concatenate(
        [dot(order, rows_ref[RAW * i : RAW * (i + 1), :]) for i in range(images)], axis=0
    )


def chunk_place(j):
    return j % 2 * 8 + j // 2 % 2 * 4 + j // 8 * 2 + j // 4 % 2


def write_chunks(outs, core, sums_ref, col):
    cols = sums_ref.shape[1]
    for j in range(sums_ref.shape[0] // 32):
        for out, bit in zip(outs, (core, 1 - core)):
            start = pl.multiple_of(16 * (2 * j + bit), 16)
            out[chunk_place(j), :, col : col + cols] = sums_ref[pl.ds(start, 16), :].astype(BF16)


def bias_kernel(code_ref, codes_ref, index_ref, table_ref, out_ref):
    out_ref[...] = jnp.full(out_ref.shape, blocked, F32)
    entry = lax.broadcasted_iota(jnp.int32, (TABLE_PAD, ROWS), 0)
    codes = codes_ref[...]
    table = table_ref[...]
    for j in range(TOKW):
        hot = (entry == index_ref[j : j + 1, :]).astype(F32).astype(BF16)
        found = dot(table, hot) * log2e
        for w in range(WINDOWS):
            row = TOKW * w + j
            out_ref[:, row, :] = jnp.where(codes == code_ref[row], found, blocked)


def table_kernel(sums_ref, index_ref, out_ref, window_ref):
    for h in range(HEADS):
        part = sums_ref[h, :TOKW, :]
        for w in range(1, WINDOWS):
            part = part + sums_ref[h, TOKW * w : TOKW * (w + 1), :]
        window_ref[h, :TOKW, :] = part
    entry = lax.broadcasted_iota(jnp.int32, (TABLE_PAD, ROWS), 0)
    total = jnp.zeros((2 * HEADS, TABLE_PAD), F32)
    for j in range(TOKW):
        part = window_ref[:, j, :]
        hot = (entry == index_ref[j : j + 1, :]).astype(F32).astype(BF16)
        high = part.astype(BF16)
        low = (part - high.astype(F32)).astype(BF16)
        total = total + dot_nt(jnp.concatenate([high, low], axis=0), hot)
    out_ref[...] = total[:HEADS] + total[HEADS:]


def attend_kernel(starts_ref, grid_ref, order_ref, rows_in_ref, bias_ref, pair_ref, *rest):
    pieces = rest[:-7]
    win_ref, in_ref, packed_ref, soft_ref, merged_ref, weight_ref, rows_ref = rest[-7:]

    @pl.when(pl.program_id(0) == 0)
    def _():
        rows = weight_ref.shape[0] // starts_ref.shape[0]
        at = 0
        for piece in pieces:
            for r in range(0, piece.shape[0], rows):
                start = pl.multiple_of(starts_ref[at], rows)
                weight_ref[pl.ds(start, rows), :] = piece[r : r + rows, :]
                at += 1

    values = load_grid(grid_ref, rows_ref, order_ref[...])
    win_ref[...] = values.astype(BF16)
    unit, _ = row_stats(values)
    attend_in = (unit * rows_in_ref[0:1, :] + rows_in_ref[1:2, :]).astype(BF16)
    in_ref[...] = attend_in
    packed_ref[...] = (dot(attend_in, weight_ref[...]) + bias_ref[...]).astype(BF16)
    for g in range(HEADS // GROUP):
        at = LANES * g
        q = packed_ref[:, at : at + LANES]
        k = packed_ref[:, C + at : C + at + LANES]
        v_turned = turned(packed_ref[:, 2 * C + at : 2 * C + at + LANES])
        raw = dot_nt(head_stack(k), q)
        parts = []
        for h in range(GROUP):
            s = raw[h * ROWS : (h + 1) * ROWS] * (scale * log2e) + pair_ref[g * GROUP + h]
            e = jnp.exp2(s - jnp.max(s, axis=0, keepdims=True))
            p = (e * (1.0 / column_sum(e))).astype(BF16)
            soft_ref[0, g * GROUP + h] = p
            parts.append(dot(v_turned[h * HEAD_DIM : (h + 1) * HEAD_DIM], p))
        merged_ref[:, at : at + LANES] = jnp.concatenate(parts, axis=0).T.astype(BF16)


def mlp_kernel(
    count_ref, win_ref, merged_ref, grid_ref, order_ref, back_ref, six_ref, exp_b_ref, joined_ref,
    block_ref, d_res_ref, d_att_ref, kept_ref, away_ref,
    sums_ref, wide_ref, rows_ref, red_w_ref, out_sum_ref, exp_sum_ref, red_sum_ref,
):
    step_at = pl.program_id(0)
    images = grid_ref.shape[0]
    out_b, gain, shift, red_b = (six_ref[r : r + 1, :] for r in (2, 3, 4, 5))
    mlp = exp_b_ref.shape[1]
    blocks = mlp // C
    out_w_ref = joined_ref.at[:, :C]
    exp_w_ref = joined_ref.at[:, C : C + mlp]

    @pl.when(step_at == 0)
    def _():
        out_sum_ref[...] = jnp.zeros_like(out_sum_ref)
        exp_sum_ref[...] = jnp.zeros_like(exp_sum_ref)
        red_sum_ref[...] = jnp.zeros_like(red_sum_ref)
        sums_ref[...] = jnp.zeros_like(sums_ref)
        wide_ref[...] = jnp.zeros_like(wide_ref)
        for at in range(0, C, 16):
            for b in range(blocks):
                cols = C + mlp + b * C
                red_w_ref[blocks * at + 16 * b : blocks * at + 16 * (b + 1), :] = joined_ref[
                    at : at + 16, cols : cols + C
                ]

    row = lax.broadcasted_iota(jnp.int32, (images * ROWS, 1), 0)
    live = (row < (count_ref[0] - images * step_at) * ROWS).astype(F32)
    grad = load_grid(grid_ref, rows_ref, order_ref[...]) * live
    grad_low = grad.astype(BF16)
    grad_turned = turned(grad_low)
    residual = win_ref[...].astype(F32) + dot(merged_ref[...], out_w_ref[...]) + out_b
    unit, inverse = row_stats(residual)
    expand_in = (unit * gain + shift).astype(BF16)
    in_turned = turned(expand_in)
    step = 512
    out = residual + red_b
    d_in = jnp.zeros((images * ROWS, C), F32)
    for m in range(0, mlp, step):
        cols = slice(m, m + step)
        pre = dot(expand_in, exp_w_ref[:, cols]) + exp_b_ref[:, cols]
        bell = jnp.exp(pre * pre * -0.5)
        t = 1.0 / (1.0 + jnp.abs(pre) * (0.3275911 * 0.7071067811865476))
        tail = (
            t
            * bell
            * (
                0.127414796
                + t * (-0.142248368 + t * (0.7107068705 + t * (-0.7265760135 + t * 0.5307027145)))
            )
        )
        cdf = jnp.where(pre >= 0, 1.0 - tail, tail)
        hidden = (pre * cdf).astype(BF16)
        red_sum_ref[:, cols] += dot(grad_turned, hidden)
        d_hidden = dot_nt(grad_low, red_w_ref[cols, :])
        d_pre = (d_hidden * (cdf + pre * bell * 0.3989422804014327)).astype(BF16)
        exp_sum_ref[:, cols] += dot(in_turned, d_pre)
        wide_ref[:, cols] += column_sum(d_pre.astype(F32))
        out = out + dot(hidden, red_w_ref[cols, :])
        d_in = d_in + dot_nt(d_pre, exp_w_ref[:, cols])
    block = (out * live).astype(BF16)
    for i in range(images):
        block_rows = dot(back_ref[...], block[ROWS * i : ROWS * (i + 1)]).astype(BF16)
        for r in range(IMG):
            block_ref[i, r] = block_rows[16 * r : 16 * r + IMG]
    d_res = grad + norm_pull(d_in, gain, unit, inverse)
    d_res_ref[...] = d_res
    d_branch = d_res.astype(BF16)
    d_att_ref[...] = dot_nt(d_branch, out_w_ref[...]).astype(BF16)
    out_sum_ref[...] += dot(turned(merged_ref[...]), d_branch)
    sums_ref[0:1, :] += column_sum(d_in * unit)
    sums_ref[1:2, :] += column_sum(d_in)
    sums_ref[2:3, :] += column_sum(d_branch.astype(F32))
    sums_ref[3:4, :] += column_sum(grad)

    @pl.when(step_at == pl.num_programs(0) - 1)
    def _():
        core = count_ref[1]
        outs = (kept_ref, away_ref)
        write_chunks(outs, core, out_sum_ref, 0)
        write_chunks(outs, core, exp_sum_ref, C)
        for m in range(0, mlp, C):
            red_w_ref[m : m + C, :] = red_sum_ref[:, m : m + C].T.astype(BF16)
        for j in range(C // 32):
            for out, bit in zip(outs, (core, 1 - core)):
                for b in range(blocks):
                    start = pl.multiple_of(16 * (blocks * (2 * j + bit) + b), 16)
                    at = C + mlp + b * C
                    out[chunk_place(j), :, at : at + C] = red_w_ref[pl.ds(start, 16), :]


def attend_back_kernel(
    core_ref, packed_ref, soft_ref, d_att_ref, in_ref,
    d_packed_ref, pairs_ref, kept_ref, away_ref, sum_ref,
):
    @pl.when(pl.program_id(0) == 0)
    def _():
        pairs_ref[...] = jnp.zeros_like(pairs_ref)
        sum_ref[...] = jnp.zeros_like(sum_ref)

    for g in range(HEADS // GROUP):
        at = LANES * g
        q = packed_ref[:, at : at + LANES]
        k_turned = turned(packed_ref[:, C + at : C + at + LANES])
        v = packed_ref[:, 2 * C + at : 2 * C + at + LANES]
        d_att = d_att_ref[:, at : at + LANES]
        d_soft = dot_nt(head_stack(v), d_att)
        d_raw, d_q, soft = [], [], []
        for h in range(GROUP):
            head = g * GROUP + h
            low = soft_ref[0, head]
            soft.append(low)
            p = low.astype(F32)
            dp = d_soft[h * ROWS : (h + 1) * ROWS]
            ds = (p * (dp - column_sum(p * dp))).astype(BF16)
            pairs_ref[head] += ds.astype(F32)
            d_raw.append(ds)
            d_q.append(dot(k_turned[h * HEAD_DIM : (h + 1) * HEAD_DIM], ds))
        d_k = head_pick(dot(jnp.concatenate(d_raw, axis=0), q))
        d_v = head_pick(dot(jnp.concatenate(soft, axis=0), d_att))
        d_packed_ref[:, at : at + LANES] = (jnp.concatenate(d_q, axis=0) * scale).T.astype(BF16)
        d_packed_ref[:, C + at : C + at + LANES] = (d_k * scale).astype(BF16)
        d_packed_ref[:, 2 * C + at : 2 * C + at + LANES] = d_v.astype(BF16)
    in_turned = turned(in_ref[...])
    for m in range(0, 3 * C, C):
        sum_ref[:, m : m + C] += dot(in_turned, d_packed_ref[:, m : m + C])

    @pl.when(pl.program_id(0) == pl.num_programs(0) - 1)
    def _():
        write_chunks((kept_ref, away_ref), core_ref[0], sum_ref, 0)


def input_kernel(
    d_packed_ref, win_ref, d_res_ref, six_ref, weight_ref, back_ref,
    grad_ref, sums_ref, wide_ref, turned_ref,
):
    @pl.when(pl.program_id(0) == 0)
    def _():
        for m in range(0, 3 * C, C):
            turned_ref[m : m + C, :] = turned(weight_ref[:, m : m + C])
        sums_ref[...] = jnp.zeros_like(sums_ref)
        wide_ref[...] = jnp.zeros_like(wide_ref)

    d_packed = d_packed_ref[...]
    d_in = dot(d_packed, turned_ref[...])
    unit, inverse = row_stats(win_ref[...].astype(F32))
    total = d_res_ref[...] + norm_pull(d_in, six_ref[0:1, :], unit, inverse)
    sums_ref[0:1, :] += column_sum(d_in * unit)
    sums_ref[1:2, :] += column_sum(d_in)
    wide_ref[...] += column_sum(d_packed.astype(F32))
    high = total.astype(BF16)
    low = (total - high.astype(F32)).astype(BF16)
    rows = dot(back_ref[...], high) + dot(back_ref[...], low)
    for r in range(IMG):
        grad_ref[0, r] = rows[16 * r : 16 * r + IMG]


def whole(shape):
    return pl.BlockSpec(shape, lambda *_: (0,) * len(shape))


def per_image(width):
    return pl.BlockSpec((ROWS, width), lambda i: (i, 0))


GRID_SPEC = pl.BlockSpec((1, IMG, IMG, C), lambda i: (i, 0, 0, 0))
SMEM_SPEC = pl.BlockSpec(memory_space=pltpu.SMEM)


def params():
    return pltpu.CompilerParams(vmem_limit_bytes=VMEM_BYTES)


def cost(flops, moved, special=0):
    return pl.CostEstimate(flops=int(flops), bytes_accessed=int(moved), transcendentals=int(special))


def struct(shape, dtype):
    return jax.ShapeDtypeStruct(shape, dtype)


def run_bias(codes, index_rows, table):
    return pl.pallas_call(
        bias_kernel,
        out_shape=struct((HEADS, ROWS, ROWS), F32),
        in_specs=[SMEM_SPEC] + [pl.BlockSpec(memory_space=pltpu.VMEM)] * 3,
        out_specs=pl.BlockSpec(memory_space=pltpu.VMEM),
        compiler_params=params(),
        cost_estimate=cost(2e9, 4e6),
    )(codes, codes[None, :], index_rows, table)


def run_table(pairs, index_rows):
    return pl.pallas_call(
        table_kernel,
        out_shape=struct((HEADS, TABLE_PAD), F32),
        in_specs=[pl.BlockSpec(memory_space=pltpu.VMEM)] * 2,
        out_specs=pl.BlockSpec(memory_space=pltpu.VMEM),
        scratch_shapes=[pltpu.VMEM((HEADS, 56, ROWS), F32)],
        compiler_params=params(),
        cost_estimate=cost(2e9, 4e6),
    )(pairs, index_rows)


def run_attend(inputs, order, six, starts, pieces, bias, pair):
    images = inputs.shape[0]
    rows = images * ROWS
    return pl.pallas_call(
        attend_kernel,
        grid=(images,),
        out_shape=(
            struct((rows, C), BF16),
            struct((rows, C), BF16),
            struct((rows, 3 * C), BF16),
            struct((images, HEADS, ROWS, ROWS), BF16),
            struct((rows, C), BF16),
            struct((C, 3 * C), BF16),
        ),
        in_specs=[
            SMEM_SPEC,
            GRID_SPEC,
            whole((ROWS, RAW)),
            whole((6, C)),
            whole((1, 3 * C)),
            whole((HEADS, ROWS, ROWS)),
        ]
        + [whole(piece.shape) for piece in pieces],
        out_specs=(
            per_image(C),
            per_image(C),
            per_image(3 * C),
            pl.BlockSpec((1, HEADS, ROWS, ROWS), lambda i: (i, 0, 0, 0)),
            per_image(C),
            whole((C, 3 * C)),
        ),
        scratch_shapes=[pltpu.VMEM((RAW, C), BF16)],
        compiler_params=params(),
        cost_estimate=cost(images * 5e9, images * 6e6),
    )(starts, inputs, order, six, bias, pair, *pieces)


def run_mlp(count, win, merged, cotangent, order, back, weights):
    images = cotangent.shape[0]
    rows = images * ROWS
    mlp = weights[1].shape[1]
    per = 2 if images % 2 == 0 else 1
    some = pl.BlockSpec((per * ROWS, C), lambda i: (i, 0))
    grids = pl.BlockSpec((per, IMG, IMG, C), lambda i: (i, 0, 0, 0))
    half = (C // 32, 16, C + 2 * mlp)
    return pl.pallas_call(
        mlp_kernel,
        grid=(images // per,),
        out_shape=(
            struct(cotangent.shape, BF16),
            struct((rows, C), F32),
            struct((rows, C), BF16),
            struct(half, BF16),
            struct(half, BF16),
            struct((8, C), F32),
            struct((1, mlp), F32),
        ),
        in_specs=[
            SMEM_SPEC,
            some,
            some,
            grids,
            whole((ROWS, RAW)),
            whole((RAW, ROWS)),
            whole((6, C)),
            whole((1, mlp)),
            whole((C, C + 2 * mlp)),
        ],
        out_specs=(grids, some, some, whole(half), whole(half), whole((8, C)), whole((1, mlp))),
        scratch_shapes=[
            pltpu.VMEM((per * RAW, C), BF16),
            pltpu.VMEM((mlp, C), BF16),
            pltpu.VMEM((C, C), F32),
            pltpu.VMEM((C, mlp), F32),
            pltpu.VMEM((C, mlp), F32),
        ],
        compiler_params=params(),
        cost_estimate=cost(images * 6e9, images * 4e6),
    )(count, win, merged, cotangent, order, back, *weights)


def run_attend_back(core, packed, soft, d_att, attend_in):
    images = soft.shape[0]
    half = (C // 32, 16, 3 * C)
    return pl.pallas_call(
        attend_back_kernel,
        grid=(images,),
        out_shape=(
            struct(packed.shape, BF16),
            struct((HEADS, ROWS, ROWS), F32),
            struct(half, BF16),
            struct(half, BF16),
        ),
        in_specs=[
            SMEM_SPEC,
            per_image(3 * C),
            pl.BlockSpec((1, HEADS, ROWS, ROWS), lambda i: (i, 0, 0, 0)),
            per_image(C),
            per_image(C),
        ],
        out_specs=(per_image(3 * C), whole((HEADS, ROWS, ROWS)), whole(half), whole(half)),
        scratch_shapes=[pltpu.VMEM((C, 3 * C), F32)],
        compiler_params=params(),
        cost_estimate=cost(images * 6e9, images * 6e6),
    )(core, packed, soft, d_att, attend_in)


def run_input(d_packed, win, d_res, six, weight, back, shape):
    return pl.pallas_call(
        input_kernel,
        grid=(shape[0],),
        out_shape=(struct(shape, F32), struct((8, C), F32), struct((1, 3 * C), F32)),
        in_specs=[
            per_image(3 * C),
            per_image(C),
            per_image(C),
            whole((6, C)),
            whole((C, 3 * C)),
            whole((RAW, ROWS)),
        ],
        out_specs=(GRID_SPEC, whole((8, C)), whole((1, 3 * C))),
        scratch_shapes=[pltpu.VMEM((3 * C, C), BF16)],
        compiler_params=params(),
        cost_estimate=cost(shape[0] * 1e9, shape[0] * 2e6),
    )(d_packed, win, d_res, six, weight, back)


def gather(shard):
    return lax.all_gather(shard, "fsdp", axis=0, tiled=True)


def images_last(grids):
    return with_layout_constraint(grids.transpose(1, 2, 0, 3), Layout((0, 1, 2, 3)))


def swap(value, axis, bits):
    return lax.ppermute(value, axis, [(i, i ^ bits) for i in range(lax.axis_size(axis))])


def pick(value, index, axis):
    return lax.dynamic_index_in_dim(value, index, axis, keepdims=False)


def gather_line(shard):
    half = shard.shape[0] // 2
    own = lax.dynamic_slice_in_dim(shard, lax.axis_index("rep") % 2 * half, half, 0)
    return jnp.concatenate([own] + [swap(own, "fsdp", d) for d in (2, 4, 6)], axis=0)


def gather_pieces(line, rows, vector_line):
    mine, core = lax.axis_index("fsdp"), lax.axis_index("rep") % 2
    across = swap(line, "fsdp", 1)
    vector = jnp.concatenate([vector_line, swap(vector_line, "fsdp", 1)], axis=0)
    across, vector = lax.optimization_barrier((across, vector))
    pieces = [line, swap(line, "rep", 1), across, swap(across, "rep", 1)]
    starts = []
    for side in (0, 1):
        for other in (0, 1):
            for d in (0, 2, 4, 6):
                starts.append((mine ^ d ^ side) * rows + (core ^ other) * (rows // 2))
    return jnp.stack(starts).astype(jnp.int32), pieces, gather_vector(vector)


def gather_vector(held):
    mine, owners = lax.axis_index("fsdp"), lax.axis_size("fsdp")
    stacked = held.reshape(owners, -1).astype(F32)
    order = jnp.asarray((0, 4, 2, 6, 1, 5, 3, 7))
    chosen = (jnp.arange(owners)[:, None] ^ order[None, :]) == mine
    return jnp.sum(jnp.where(chosen[:, :, None], stacked[None], 0.0), axis=1)


def gather_joined(weight_out, weight_exp, weight_red):
    replica, replicas = lax.axis_index("rep"), lax.axis_size("rep")
    rows = weight_out.shape[0] // replicas
    blocks = weight_red.shape[0] // weight_out.shape[0]

    def quarter(shard):
        size = shard.shape[0] // replicas
        return lax.dynamic_slice_in_dim(shard, replica * size, size, 0)

    red = quarter(weight_red).reshape(blocks, rows, C).transpose(1, 0, 2).reshape(rows, blocks * C)
    joined = jnp.concatenate([quarter(weight_out), quarter(weight_exp), red], axis=1)
    return lax.all_gather(joined, ("fsdp", "rep"), axis=0, tiled=True)


def halves(block, bit, axis):
    return pick(block, bit, axis), pick(block, 1 - bit, axis)


def added(a, b):
    return (a.astype(F32) + b.astype(F32)).astype(BF16)


def chunk_rows(kept, away):
    chunks = jnp.stack([kept, away]).reshape(2, 2, 2, 2, 2, 16, -1)
    return chunks.transpose(3, 4, 2, 1, 0, 5, 6).reshape(C, -1)


def scatter_bits():
    mine, replica = lax.axis_index("fsdp"), lax.axis_index("rep")
    return mine // 4, mine // 2 % 2, mine % 2, replica // 2, replica % 2


def scatter_plane(kept, got, row, side):
    parts = []
    for far_row, far_side in ((0, 0), (1, 0), (0, 1), (1, 1)):
        at = [pick(pick(part, row ^ far_row, 0), side ^ far_side, 0) for part in (kept, got)]
        parts.append(added(*at))
    return parts


def scatter_step(kept, got, bit):
    keep, away = halves(kept, bit, 0)
    got_keep, got_away = halves(got, bit, 0)
    return added(keep, got_keep), added(away, got_away)


def join_kernel(ids_ref, both_ref, rest_ref, *refs):
    parts, rows_ref = refs[:4], refs[4]
    outs, vectors = refs[5:9], refs[9:]
    at = 0
    for out in outs:
        rows, cols = out.shape
        rows = rows // 4
        for e in range(4):
            start = pl.multiple_of((ids_ref[0] ^ e) * rows, rows)
            for b in range(rows // 16):
                if out is outs[3]:
                    block = parts[e][...]
                else:
                    block = (both_ref, rest_ref)[e // 2][e % 2, :, at + b * cols : at + (b + 1) * cols]
                out[pl.ds(start + 16 * b, 16), :] = block.astype(F32)
        at += rows // 16 * cols
    mine = ids_ref[1]
    base = 0
    for vector in vectors:
        if vector.shape[1] < 128:
            row = rows_ref[pl.ds(base + mine // 2, 1), :]
            moved = jnp.concatenate([row[:, 64:], row[:, :64]], axis=1)
            vector[...] = jnp.where(mine % 2 == 1, moved, row)[:, :64]
            base += 4
        else:
            count = vector.shape[0]
            for r in range(count):
                vector[r : r + 1, :] = rows_ref[pl.ds(base + count * mine + r, 1), :]
            base += 8 * count


def run_join(mlp, parts, rows, shapes, sizes):
    ids = jnp.stack([lax.axis_index("rep"), lax.axis_index("fsdp")]).astype(jnp.int32)
    moved = sum(6 * a * b for a, b in shapes)
    flat = [(max(size // 128, 1), min(size, 128)) for size in sizes]
    count = len(shapes) + len(sizes)
    outs = pl.pallas_call(
        join_kernel,
        out_shape=[struct(shape, F32) for shape in list(shapes) + flat],
        in_specs=[SMEM_SPEC] + [pl.BlockSpec(memory_space=pltpu.VMEM)] * 7,
        out_specs=[pl.BlockSpec(memory_space=pltpu.VMEM)] * count,
        compiler_params=params(),
        cost_estimate=cost(moved, moved),
    )(ids, *mlp, *parts, rows)
    return outs[:4], [out.reshape(-1) for out in outs[4:]]


def finish(kept_mlp, got_mlp, kept, got, vector, result):
    _, near, side, _, _ = scatter_bits()
    line = lax.axis_index("fsdp") // 2
    tie = lax.optimization_barrier
    kept_mlp, got_mlp, kept, got, vector = tie((kept_mlp, got_mlp, kept, got, vector))
    kept_mlp, away_mlp = scatter_step(kept_mlp, got_mlp, near)
    kept, away = scatter_step(kept, got, side)
    rows = jnp.pad(jnp.concatenate(vector), (0, -sum(v.shape[0] for v in vector) % 1024))
    rows = rows.reshape(-1, 128)

    away_mlp, away, rows = tie((away_mlp, away, rows))
    total_mlp = added(kept_mlp, swap(away_mlp, "fsdp", 2))
    total = added(kept, swap(away, "fsdp", 1)).reshape(4, kept.shape[-2], kept.shape[-1])
    own = pick(total, line, 0)
    pieces = [pick(total, line ^ d, 0) for d in (1, 2, 3)]
    rows = rows + swap(rows, "rep", 1)

    own, pieces, total_mlp, rows = tie((own, pieces, total_mlp, rows))
    result = images_last(result)
    total = own.astype(F32)
    for d in (1, 2, 3):
        total = total + swap(pieces[d - 1], "fsdp", 2 * d).astype(F32)
    total = total.astype(BF16)
    both_mlp = jnp.stack([total_mlp, swap(total_mlp, "rep", 1)])
    rows = rows + swap(rows, "rep", 2)
    rows = rows + swap(rows, "fsdp", 1)

    total, both_mlp, rows, result = tie((total, both_mlp, rows, result))
    parts = [total] + [swap(total, "rep", e) for e in (1, 2, 3)]
    rest_mlp = swap(both_mlp, "rep", 2)
    rows = rows + swap(rows, "fsdp", 4)
    rows = rows + swap(rows, "fsdp", 2)
    return [both_mlp, rest_mlp], parts, rows, result.transpose(2, 0, 1, 3)


def reduce_weight_grad(partial):
    share = lax.psum_scatter(partial, "fsdp", scatter_dimension=0, tiled=True)
    return lax.psum(share, "rep").astype(F32)


def per_device(
    inputs,
    cotangent,
    image_counts,
    region_labels,
    position_index,
    first_gain,
    first_shift,
    attend_weight,
    attend_bias,
    bias_table,
    output_weight,
    output_bias,
    second_gain,
    second_shift,
    expand_weight,
    expand_bias,
    reduce_weight,
    reduce_bias,
):
    order_host = window_order()
    order = jnp.asarray(order_host, BF16)
    back = jnp.asarray(order_host.T, BF16)
    shards = lax.axis_size("fsdp")
    mine = lax.axis_index("fsdp")
    paired = shards == 8 and lax.axis_size("rep") == 4

    window_of = jnp.arange(WINDOWS, dtype=jnp.int32)[:, None]
    codes = jnp.pad(
        (region_labels + 4 * window_of).reshape(-1), (0, ROWS - TOK), constant_values=-1
    )
    index_rows = jnp.pad(jnp.tile(position_index.T, (1, WINDOWS)), ((0, 0), (0, ROWS - TOK)))
    table = jnp.pad(bias_table.T, ((0, 0), (0, TABLE_PAD - TABLE)))
    vectors = (
        first_gain, first_shift, output_bias, second_gain, second_shift, reduce_bias,
        attend_bias, expand_bias,
    )
    sizes = [v.shape[0] for v in vectors]
    if paired:
        joined_weights = gather_joined(output_weight, expand_weight, reduce_weight)
        line = gather_line(attend_weight)
        own = jnp.concatenate(vectors).reshape(1, -1, 128)
        vector_line = jnp.concatenate([own, swap(own, "fsdp", 4)], axis=0)
        line, vector_line, codes = lax.optimization_barrier((line, vector_line, codes))
        vector_line = jnp.concatenate([vector_line, swap(vector_line, "fsdp", 2)], axis=0)
        starts, pieces, joined = gather_pieces(line, attend_weight.shape[0], vector_line)
        inputs, cotangent, _ = lax.optimization_barrier((inputs, cotangent, line))
    else:
        joined = gather(jnp.concatenate(vectors)).reshape(shards, sum(sizes)).astype(F32)
    pair = run_bias(codes, index_rows, table)
    pair = run_bias(codes, index_rows, table)
    six = joined[:, : 6 * sizes[0]].reshape(shards, 6, sizes[0]).transpose(1, 0, 2).reshape(6, C)
    bias_one = joined[:, 6 * sizes[0] : 6 * sizes[0] + sizes[6]].reshape(1, 2 * C)
    bias_exp = joined[:, 6 * sizes[0] + sizes[6] :].reshape(1, shards * sizes[7])
    bias_packed = jnp.concatenate(
        [bias_one[:, :C], jnp.zeros((1, C), F32), bias_one[:, C:]], axis=1
    )
    if not paired:
        starts, pieces = jnp.zeros((1,), jnp.int32), [gather(attend_weight)]
        red = gather(reduce_weight).reshape(C // 16, -1, 16, C).transpose(0, 2, 1, 3).reshape(C, -1)
        joined_weights = jnp.concatenate([gather(output_weight), gather(expand_weight), red], axis=1)

    win, attend_in, packed, soft, merged, weight_one = run_attend(
        inputs, order, six, starts, pieces, bias_packed, pair
    )
    far, _, side, row, core = scatter_bits()
    core = core if paired else jnp.zeros((), jnp.int32)
    block_output, d_res, d_att, kept_mlp, away_mlp, sums_two, d_exp_bias = run_mlp(
        jnp.stack([image_counts[0, 0], core]), win, merged, cotangent, order, back,
        (six, bias_exp, joined_weights),
    )
    tie = lax.optimization_barrier
    if paired:
        split = (2, 2, 2, 2, 16, -1)
        got = swap(away_mlp.reshape(split), "rep", 1)
        plane = scatter_plane(kept_mlp.reshape(split), got, row, side)
        d_att, plane, block_output = tie((d_att, plane, images_last(block_output)))
        block_output = block_output.transpose(2, 0, 1, 3)
        plane = [
            plane[0],
            swap(plane[1], "rep", 2),
            swap(plane[2], "fsdp", 1),
            swap(plane[3], ("fsdp", "rep"), lax.axis_size("rep") + 2),
        ]
    d_packed, pairs, kept, away = run_attend_back(core[None], packed, soft, d_att, attend_in)
    if paired:
        halved = [halves(part, far, 0) for part in plane]
        kept_mlp, away_mlp = (
            sum(half[at].astype(F32) for half in halved).astype(BF16) for at in (0, 1)
        )
        pairs, away, away_mlp = tie((pairs, away, away_mlp))
        kept, away = kept.reshape(split), away.reshape(split)
        got, got_mlp = swap(away, "rep", 1), swap(away_mlp, "fsdp", 4)
    table_part = run_table(pairs, index_rows)
    if paired:
        kept, away = scatter_step(kept, got, row)
        d_packed, away, table_part = lax.optimization_barrier((d_packed, away, table_part))
        got = swap(away, "rep", 2)
    input_grad, sums_one, d_packed_bias = run_input(
        d_packed, win, d_res, six, weight_one, back, inputs.shape
    )
    small = (
        sums_one[0], sums_one[1], sums_two[2], sums_two[0], sums_two[1], sums_two[3],
        d_packed_bias[0, :C], d_packed_bias[0, 2 * C :], d_exp_bias[0], table_part.reshape(-1),
    )
    if paired:
        mlp_pieces, part_pieces, rows, input_grad = finish(
            kept_mlp, got_mlp, kept, got, small, input_grad
        )
        (output_grad, expand_grad, reduce_grad, attend_grad), owned = run_join(
            mlp_pieces, part_pieces, rows,
            [w.shape for w in (output_weight, expand_weight, reduce_weight, attend_weight)],
            sizes,
        )
        table_sum = rows.reshape(-1)[sum(sizes) * shards :][: HEADS * TABLE_PAD]
    else:
        parts = chunk_rows(kept_mlp, away_mlp)
        mlp = bias_exp.shape[1]
        reduce_part = parts[:, C + mlp :].reshape(C // 16, 16, -1, C).transpose(0, 2, 1, 3)
        output_grad, expand_grad, attend_grad, reduce_grad = (
            reduce_weight_grad(part)
            for part in (
                parts[:, :C], parts[:, C : C + mlp], chunk_rows(kept, away), reduce_part.reshape(mlp, C),
            )
        )
        summed = lax.psum(jnp.concatenate(small), ("fsdp", "rep"))
        ends = np.cumsum([0] + [size * shards for size in sizes])
        owned = [
            lax.dynamic_slice(summed[ends[i] : ends[i + 1]], (mine * sizes[i],), (sizes[i],))
            for i in range(len(sizes))
        ]
        table_sum = summed[ends[-1] :]
    table_grad = table_sum.reshape(HEADS, TABLE_PAD)[:, :TABLE].T
    return (
        block_output,
        input_grad,
        owned[0],
        owned[1],
        attend_grad,
        owned[6],
        table_grad,
        output_grad,
        owned[2],
        owned[3],
        owned[4],
        expand_grad,
        owned[7],
        reduce_grad,
        owned[5],
    )


def solution(mesh):
    images = P(("fsdp", "rep"), None, None, None)
    rows, vector = P("fsdp", None), P("fsdp")
    return jax.shard_map(
        per_device,
        mesh=mesh,
        in_specs=(
            images, images, P("fsdp", "rep"), P(), P(), vector, vector, rows, vector, P(),
            rows, vector, vector, vector, rows, vector, rows, vector,
        ),
        out_specs=(
            images, images, vector, vector, rows, vector, P(), rows, vector, vector, vector,
            rows, vector, rows, vector,
        ),
        check_vma=False,
    )
```
